256 devices in a mesh: zero: 64 (over x, z, core), tensor: 4 (over y).
Axes of the slice: x: 4, y: 4, z: 8, core: 2. Of those that a mesh axis runs over, the one named last changes fastest.
Arguments:
- momentum: bfloat16 [28672, 8192], P('zero', 'tensor'), may hold values from -12 to 12
- gradient: bfloat16 [28672, 8192], P('zero', 'tensor'), may hold values from -12 to 12
- old_basis: bfloat16 [8192, 512], P('tensor'), may hold values from -4 to 4
Outputs:
- new_momentum: bfloat16 [28672, 8192], P('zero', 'tensor')
- new_basis: bfloat16 [8192, 512], P('tensor')
- direction: bfloat16 [28672, 8192], P('zero', 'tensor')
The draws below stay inside these ranges and needn't reach their ends.
All inputs are finite; a program needn't handle non-finite values.
Results may differ from the reference program's by a relative error of at most 0.023.
Values may be sent and summed in bfloat16 or wider, within the bound.
A program may use at most 64 MiB of HBM per device.

```python
import math
import jax
import jax.numpy as jnp
from jax import lax

ROWS = 28672
COLS = 8192
RANK = 512


def column_scales(key):
    column_key = jax.random.fold_in(key, 7)
    return jnp.exp(jax.random.uniform(column_key, (COLS,), jnp.float32, math.log(0.1), math.log(3.0)))


def scaled_entries(key, scales):
    entries = jax.random.truncated_normal(key, -4.0, 4.0, (ROWS, COLS), jnp.float32)
    return entries * scales[None, :]


def draw_momentum(key, part):
    scales = column_scales(key)
    key = jax.random.fold_in(key, 1)
    return scaled_entries(key, scales).astype(jnp.bfloat16)


def draw_gradient(key, part):
    scales = column_scales(key)
    key = jax.random.fold_in(key, 2)
    return scaled_entries(key, scales).astype(jnp.bfloat16)


def shard_levels(stream_key, dims, pieces, smallest, largest):
    loudness, own = 1.0, jax.random.fold_in(stream_key, 6)
    for dim, shards_of in pieces:
        draws = jnp.exp(jax.random.uniform(jax.random.fold_in(own, dim), (shards_of,), jnp.float32, smallest / len(pieces), largest / len(pieces)))
        loudness = loudness * jnp.repeat(draws, dims[dim] // shards_of).reshape([-1 if axis == dim else 1 for axis in range(len(dims))])
    return loudness


def gaussian(key, dims, width, reach, shards=(), kind=jnp.bfloat16):
    array = width * jax.random.normal(key, dims, jnp.float32)
    if shards:
        array = array * shard_levels(key, dims, shards, -0.22, 0.18)
    return jnp.clip(array, -reach, reach).astype(kind)


def setup_inputs(seed: int = 0) -> dict:
    keys = jax.random.split(jax.random.key(seed), 4)
    momentum = draw_momentum(jax.random.fold_in(keys[3], 71), 0)
    gradient = draw_gradient(jax.random.fold_in(keys[3], 71), 0)
    old_basis = gaussian(keys[2], (COLS, RANK), 1.0, 4.0, ((0, 4),))
    return {"momentum": momentum, "gradient": gradient, "old_basis": old_basis}


def reference(momentum, gradient, old_basis):
    buffer = (momentum.astype(jnp.float32) + gradient.astype(jnp.float32)).astype(jnp.bfloat16)
    projected = jnp.dot(buffer.astype(jnp.float32), old_basis.astype(jnp.float32), preferred_element_type=jnp.float32)
    gram_sum = jnp.dot(projected.T, projected, precision=lax.Precision.HIGHEST)
    factor_low = jnp.linalg.cholesky(gram_sum)
    orthonormal = lax.linalg.triangular_solve(factor_low, projected, left_side=False, lower=True, transpose_a=True).astype(jnp.bfloat16)
    r_whole = jnp.dot(buffer.T.astype(jnp.float32), orthonormal.astype(jnp.float32), preferred_element_type=jnp.float32)
    r_rounded = r_whole.astype(jnp.bfloat16)
    col_scale = lax.rsqrt(lax.optimization_barrier(jnp.mean(r_whole * r_whole, axis=0)) + 1e-06)
    new_basis = (r_whole * col_scale).astype(jnp.bfloat16)
    low_rank = jnp.dot(orthonormal.astype(jnp.float32), r_rounded.T.astype(jnp.float32), preferred_element_type=jnp.float32)
    new_momentum = (buffer.astype(jnp.float32) - 0.05 * low_rank).astype(jnp.bfloat16)
    update = jnp.dot(orthonormal.astype(jnp.float32), new_basis.T.astype(jnp.float32), preferred_element_type=jnp.float32)
    direction = (math.sqrt(ROWS / RANK) * update).astype(jnp.bfloat16)
    return (new_momentum, new_basis, direction)
```

```python
import functools
import math

import jax
import jax.numpy as jnp
from jax import lax
from jax.experimental import pallas as pl
from jax.experimental.pallas import tpu as pltpu
from jax.sharding import PartitionSpec as P

ROWS = 28672
COLS = 8192
RANK = 512
F32 = jnp.float32
BF16 = jnp.bfloat16
HIGHEST = lax.Precision.HIGHEST
SHAPE = (4, 8, 4)
VMEM_LIMIT = 56 * 1024 * 1024


def dot(a, b, contract=((1,), (0,)), precision=None):
    return lax.dot_general(
        a, b, (contract, ((), ())), precision=precision, preferred_element_type=F32
    )


def reduce_kernel(shape, mom, grad, basis, p_out, g_out, t_out, buf, p_part, p_rx, p_t,
                  g_send, g_own, g_core, g_xs, g_xrx, g_zs, g_zrx,
                  t_send, t_own, t_core, t_xs, t_xrx, t_zs, t_zrx,
                  core_s, core_r, x_s, x_r, y_s, y_r, z_s, z_r):
    nx, nz, ny = shape
    zero, y = lax.axis_index("zero"), lax.axis_index("tensor")
    c = lax.rem(zero, 2)
    z = lax.rem(lax.div(zero, 2), nz)
    x = lax.div(zero, 2 * nz)
    other = 1 - c

    def at(xx, zz, cc):
        return (xx * nz + zz) * 2 + cc

    def hop(axis, d):
        if axis == "x":
            return (at(lax.rem(x + d, nx), z, c), y)
        if axis == "z":
            return (at(x, lax.rem(z + d, nz), c), y)
        if axis == "y":
            return (zero, lax.rem(y + d, ny))
        return (at(x, z, other), y)

    def copy(src, dst, send, recv, device):
        return pltpu.make_async_remote_copy(
            src_ref=src, dst_ref=dst, send_sem=send, recv_sem=recv,
            device_id=device, device_id_type=pl.DeviceIdType.MESH)

    barrier = pltpu.get_barrier_semaphore()
    peers = [hop("y", d) for d in range(1, ny)] + [hop("x", d) for d in range(1, nx)]
    peers += [hop("z", d) for d in range(1, nz)] + [hop("core", 1)]
    for peer in peers:
        pl.semaphore_signal(barrier, inc=1, device_id=peer, device_id_type=pl.DeviceIdType.MESH)

    pending = []

    def partial_rows(u):
        rows = (mom[u].astype(F32) + grad[u].astype(F32)).astype(BF16)
        buf[u] = rows
        return dot(rows, basis[...])

    order = sorted(range(1, ny), key=lambda d: -min(d, ny - d))
    started = {}
    for n, d in enumerate(order):
        u = lax.rem(y + d, ny)
        p_part[d - 1] = partial_rows(u).astype(BF16)
        if n == 0:
            pl.semaphore_wait(barrier, len(peers))
        started[d] = copy(p_part.at[d - 1], p_rx.at[d - 1], y_s.at[0, d - 1], y_r.at[0, d - 1], hop("y", d))
        started[d].start()
    own = partial_rows(y)
    for d in order:
        started[d].wait_recv()
        own = own + p_rx[d - 1].astype(F32)
    p_out[y] = own.astype(BF16)
    pending += started.values()
    gathers = []
    for d in order:
        go = copy(p_out.at[y], p_out.at[y], y_s.at[1, d - 1], y_r.at[1, d - 1], hop("y", d))
        go.start()
        gathers.append(go)

    def finish_gather(axis, n, view, copies, sems):
        me, size = {"x": (x, nx), "y": (y, ny), "z": (z, nz)}[axis]
        for d in range(1, size):
            src = lax.rem(me - d + size, size)
            copy(view(src), view(src), sems[0].at[n, d - 1], sems[1].at[n, d - 1], hop(axis, d)).wait_recv()
        pending.extend(copies)

    def start_gather(axis, n, view, sems):
        me, size = {"x": (x, nx), "y": (y, ny), "z": (z, nz)}[axis]
        copies = []
        for d in sorted(range(1, size), key=lambda d: -min(d, size - d)):
            go = copy(view(me), view(me), sems[0].at[n, d - 1], sems[1].at[n, d - 1], hop(axis, d))
            go.start()
            copies.append(go)
        return copies

    def start_scatter(axis, n, send, rx, sems):
        me, size = {"x": (x, nx), "y": (y, ny), "z": (z, nz)}[axis]
        copies = []
        for d in sorted(range(1, size), key=lambda d: -min(d, size - d)):
            go = copy(send.at[lax.rem(me + d, size)], rx.at[d - 1], sems[0].at[n, d - 1], sems[1].at[n, d - 1], hop(axis, d))
            go.start()
            copies.append(go)
        return copies

    def end_scatter(copies):
        for go in copies:
            go.wait_recv()
        pending.extend(copies)

    xs, ys, zs = (x_s, x_r), (y_s, y_r), (z_s, z_r)
    finish_gather("y", 1, lambda i: p_out.at[i], gathers, ys)

    rows, rank = buf.shape[0] * buf.shape[1], p_out.shape[2]
    half = rank // 2
    p_all = p_out[...].reshape(rows, rank)
    p_t[...] = p_all.T.reshape(2, half, rows)
    gcols = rank // ny

    p_cols = [p_all[:, gcols * i: gcols * (i + 1)] for i in range(ny)]
    p_mine = p_cols[0]
    for i in range(1, ny):
        p_mine = jnp.where(y == i, p_cols[i], p_mine)
    g_send[...] = dot(p_t[other], p_mine).reshape(g_send.shape)
    g_go = copy(g_send, g_core, core_s.at[0], core_r.at[0], hop("core", 1))
    g_go.start()
    g_own[...] = dot(p_t[c], p_mine).reshape(g_own.shape)

    cb = t_send.shape[3]
    for k in range(nz):
        cols = buf[:, :, cb * k: cb * (k + 1)].reshape(rows, cb)
        t_send[:, k] = dot(p_t[other], cols).astype(BF16).reshape(t_send.shape[0], t_send.shape[2], cb)
    t_go = []
    for i in range(nx):
        go = copy(t_send.at[i], t_core.at[i], core_s.at[1 + i], core_r.at[1 + i], hop("core", 1))
        go.start()
        t_go.append(go)
    for k in range(nz):
        cols = buf[:, :, cb * k: cb * (k + 1)].reshape(rows, cb)
        t_own[:, k] = dot(p_t[c], cols).reshape(t_send.shape[0], t_send.shape[2], cb)

    g_go.wait_recv()
    g_xs[...] = g_own[...] + g_core[...]
    g_x = start_scatter("x", 0, g_xs, g_xrx, xs)
    for i in range(nx):
        t_go[i].wait_recv()
    pending += [g_go, *t_go]

    def add_core(i, carry):
        total = t_own[i] + t_core[i].astype(F32)
        t_own[i] = total
        t_xs[i] = total.astype(BF16)
        return carry

    lax.fori_loop(0, nx, add_core, 0)
    t_x = start_scatter("x", 1, t_xs, t_xrx, xs)

    end_scatter(g_x)
    g_zs[...] = sum((g_xrx[d] for d in range(nx - 1)), g_xs[x])
    g_z = start_scatter("z", 0, g_zs, g_zrx, zs)
    end_scatter(t_x)

    def add_x(k, carry):
        total = t_own[x, k]
        for d in range(nx - 1):
            total = total + t_xrx[d, k].astype(F32)
        t_own[x, k] = total
        t_zs[k] = total.astype(BF16)
        return carry

    lax.fori_loop(0, nz, add_x, 0)
    t_z = start_scatter("z", 1, t_zs, t_zrx, zs)

    end_scatter(g_z)
    g_out[c, x, y, z] = sum((g_zrx[d] for d in range(nz - 1)), g_zs[z])
    g_gz = start_gather("z", 2, lambda i: g_out.at[c, x, y, i], zs)
    end_scatter(t_z)
    t_out[c, x, z] = sum((t_zrx[d].astype(F32) for d in range(nz - 1)), t_own[x, z]).astype(BF16)
    t_gz = start_gather("z", 3, lambda i: t_out.at[c, x, i], zs)

    finish_gather("z", 2, lambda i: g_out.at[c, x, y, i], g_gz, zs)
    g_gy = start_gather("y", 2, lambda i: g_out.at[c, x, i], ys)
    finish_gather("z", 3, lambda i: t_out.at[c, x, i], t_gz, zs)
    t_gx = start_gather("x", 2, lambda i: t_out.at[c, i], xs)
    finish_gather("y", 2, lambda i: g_out.at[c, x, i], g_gy, ys)
    g_gx = start_gather("x", 3, lambda i: g_out.at[c, i], xs)
    finish_gather("x", 2, lambda i: t_out.at[c, i], t_gx, xs)
    t_gc = copy(t_out.at[c], t_out.at[c], core_s.at[nx + 1], core_r.at[nx + 1], hop("core", 1))
    t_gc.start()
    finish_gather("x", 3, lambda i: g_out.at[c, i], g_gx, xs)
    g_gc = copy(g_out.at[c], g_out.at[c], core_s.at[nx + 2], core_r.at[nx + 2], hop("core", 1))
    g_gc.start()
    copy(t_out.at[other], t_out.at[other], core_s.at[nx + 1], core_r.at[nx + 1], hop("core", 1)).wait_recv()
    copy(g_out.at[other], g_out.at[other], core_s.at[nx + 2], core_r.at[nx + 2], hop("core", 1)).wait_recv()
    pending += [t_gc, g_gc]
    for go in pending:
        go.wait_send()


def reduce_call(shape, mom, grad, basis):
    nx, nz, ny = shape
    rows, cols = mom.shape
    rank = basis.shape[1]
    part, cb, rb, gb = rows // ny, cols // nz, rank // (2 * nx), rank // (2 * nx * nz)
    gc = rank // ny
    vmem, sem = pltpu.VMEM, pltpu.SemaphoreType.DMA
    space = pl.BlockSpec(memory_space=pltpu.VMEM)
    return pl.pallas_call(
        functools.partial(reduce_kernel, shape),
        out_shape=(
            jax.ShapeDtypeStruct((ny, part, rank), BF16),
            jax.ShapeDtypeStruct((2, nx, ny, nz, gb, gc), F32),
            jax.ShapeDtypeStruct((2, nx, nz, rb, cb), BF16),
        ),
        in_specs=[space] * 3,
        out_specs=(space,) * 3,
        scratch_shapes=[
            vmem((ny, part, cols), BF16),
            vmem((ny - 1, part, rank), BF16),
            vmem((ny - 1, part, rank), BF16),
            vmem((2, rank // 2, rows), BF16),
            vmem((nx, nz, gb, gc), F32),
            vmem((nx, nz, gb, gc), F32),
            vmem((nx, nz, gb, gc), F32),
            vmem((nx, nz, gb, gc), F32),
            vmem((nx - 1, nz, gb, gc), F32),
            vmem((nz, gb, gc), F32),
            vmem((nz - 1, gb, gc), F32),
            vmem((nx, nz, rb, cb), BF16),
            vmem((nx, nz, rb, cb), F32),
            vmem((nx, nz, rb, cb), BF16),
            vmem((nx, nz, rb, cb), BF16),
            vmem((nx - 1, nz, rb, cb), BF16),
            vmem((nz, rb, cb), BF16),
            vmem((nz - 1, rb, cb), BF16),
            sem((nx + 3,)), sem((nx + 3,)),
            sem((4, nx - 1)), sem((4, nx - 1)),
            sem((3, ny - 1)), sem((3, ny - 1)),
            sem((4, nz - 1)), sem((4, nz - 1)),
        ],
        compiler_params=pltpu.CompilerParams(
            collective_id=0, has_side_effects=True, vmem_limit_bytes=VMEM_LIMIT),
        name="reduce",
    )(mom.reshape(ny, part, cols), grad.reshape(ny, part, cols), basis)


def factor8(cols):
    e = [[jnp.broadcast_to(cols[k][q:q + 1, :], (8, 128)) for k in range(q + 1)] for q in range(8)]
    low = [[None] * 8 for _ in range(8)]
    inv = [[None] * 8 for _ in range(8)]
    for p in range(8):
        inv[p][p] = lax.rsqrt(e[p][p])
        for q in range(p + 1, 8):
            low[q][p] = e[q][p] * inv[p][p]
        for q in range(p + 1, 8):
            for k in range(p + 1, q + 1):
                e[q][k] = e[q][k] - low[q][p] * low[k][p]
    for q in range(8):
        for k in range(q):
            acc = low[q][k] * inv[k][k]
            for m in range(k + 1, q):
                acc = acc + low[q][m] * inv[m][k]
            inv[q][k] = -acc * inv[q][q]
    return inv


def lanes(x, k):
    return jnp.broadcast_to(x[:, k:k + 1], (8, 128))


def rows8(x, k):
    return jnp.broadcast_to(x[k:k + 1, :], (8, 128))


def factor128(r):
    sub = lax.broadcasted_iota(jnp.int32, (8, 128), 0)
    for s in range(16):
        lo = 8 * s
        a, v = r[lo:lo + 8, 0:128], r[lo:lo + 8, 128:256]
        cols = [lanes(a, lo + k) for k in range(8)]
        if s < 15:
            an, vn = r[lo + 8:lo + 16, 0:128], r[lo + 8:lo + 16, 128:256]
            nxt = [lanes(an, lo + k) for k in range(8)]
        inv = factor8(cols)
        new_a = new_v = None
        for k in range(8):
            m = jnp.where(sub == k, inv[k][k], 0.0)
            for q in range(k + 1, 8):
                m = jnp.where(sub == q, inv[q][k], m)
            ta, tv = m * rows8(a, k), m * rows8(v, k)
            new_a = ta if new_a is None else new_a + ta
            new_v = tv if new_v is None else new_v + tv
        r[lo:lo + 8, 128:256] = new_v
        if s < 15:
            for k in range(8):
                lc = nxt[0] * inv[k][0]
                for j in range(1, k + 1):
                    lc = lc + nxt[j] * inv[k][j]
                an = an - lc * rows8(new_a, k)
                vn = vn - lc * rows8(new_v, k)
            r[lo + 8:lo + 16, 0:128], r[lo + 8:lo + 16, 128:256] = an, vn
        if s < 14:
            both = jnp.concatenate([new_a, new_v], axis=1)
            update = dot(new_a, both, ((0,), (0,)), HIGHEST)
            r[lo + 16:128, :] = r[lo + 16:128, :] - update[lo + 16:128, :]


def split(x):
    high = x.astype(BF16)
    return high, (x - high.astype(F32)).astype(BF16)


def factor_kernel(p_ref, g_ref, t_ref, orth_ref, r_ref, sq_ref, m, w):
    rank = m.shape[0]
    nb = rank // 128
    for i in range(2):
        for j in range(g_ref.shape[1]):
            for k in range(g_ref.shape[2]):
                rows = g_ref.shape[3] * g_ref.shape[4]
                lo = (i * g_ref.shape[1] + j) * rows
                m[lo:lo + rows, 128 * k:128 * (k + 1)] = g_ref[i, j, k].reshape(rows, 128)
    row = lax.broadcasted_iota(jnp.int32, (128, 128), 0)
    col = lax.broadcasted_iota(jnp.int32, (128, 128), 1)
    eye = jnp.where(row == col, 1.0, 0.0)
    for i in range(nb):
        for j in range(nb):
            m[128 * i:128 * (i + 1), rank + 128 * j:rank + 128 * (j + 1)] = eye if i == j else jnp.zeros_like(eye)
    for k in range(nb):
        lo, hi = 128 * k, 128 * (k + 1)
        w[:, 0:128] = m[lo:hi, lo:hi]
        w[:, 128:256] = eye
        factor128(w)
        inv = w[:, 128:256]
        m[lo:hi, hi:rank + hi] = dot(inv, m[lo:hi, hi:rank + hi], precision=HIGHEST)
        if k + 1 < nb:
            m[hi:, hi:rank + hi] = m[hi:, hi:rank + hi] - dot(
                m[lo:hi, hi:rank], m[lo:hi, hi:rank + hi], ((0,), (0,)), HIGHEST)
    high, low = split(m[:, rank:])
    rows = p_ref.shape[0] * p_ref.shape[1]
    p_all = p_ref[...].reshape(rows, rank)
    orth_ref[...] = (dot(p_all, high, ((1,), (1,))) + dot(p_all, low, ((1,), (1,)))).astype(BF16)
    nz, cb = t_ref.shape[2], t_ref.shape[4]
    total = jnp.zeros((rank, 128), F32)
    for k in range(nz):
        t = t_ref[:, :, k].reshape(rank, cb)
        r = dot(high, t) + dot(low, t)
        r_ref[:, cb * k:cb * (k + 1)] = r
        sq = r * r
        for i in range(cb // 128):
            total = total + sq[:, 128 * i:128 * (i + 1)]
    sq_ref[...] = jnp.sum(total, axis=1, keepdims=True)


def factor_call(p_sum, gram, t_sum):
    rows, rank = p_sum.shape[0] * p_sum.shape[1], p_sum.shape[2]
    cols = t_sum.shape[2] * t_sum.shape[4]
    space = pl.BlockSpec(memory_space=pltpu.VMEM)
    return pl.pallas_call(
        factor_kernel,
        out_shape=(
            jax.ShapeDtypeStruct((rows, rank), BF16),
            jax.ShapeDtypeStruct((rank, cols), F32),
            jax.ShapeDtypeStruct((rank, 1), F32),
        ),
        in_specs=[space] * 3,
        out_specs=(space,) * 3,
        scratch_shapes=[pltpu.VMEM((rank, 2 * rank), F32), pltpu.VMEM((128, 256), F32)],
        compiler_params=pltpu.CompilerParams(vmem_limit_bytes=VMEM_LIMIT),
        name="factor",
    )(p_sum, gram, t_sum)


def per_device(momentum, gradient, old_basis):
    p_sum, gram, t_sum = reduce_call(SHAPE, momentum, gradient, old_basis)
    orthonormal, r_t, squares = factor_call(p_sum, gram, t_sum)
    col_squares = lax.psum(squares, "tensor")
    col_scale = lax.rsqrt(col_squares / COLS + 1e-06)
    buffer = (momentum.astype(F32) + gradient.astype(F32)).astype(BF16)
    low_rank = dot(orthonormal, r_t.astype(BF16))
    new_momentum = (buffer.astype(F32) - 0.05 * low_rank).astype(BF16)
    basis_t = (r_t * col_scale).astype(BF16)
    direction = (math.sqrt(ROWS / RANK) * dot(orthonormal, basis_t)).astype(BF16)
    return (new_momentum, basis_t.T, direction)


def solution(mesh):
    in_specs = (P("zero", "tensor"), P("zero", "tensor"), P("tensor", None))
    out_specs = (P("zero", "tensor"), P("tensor", None), P("zero", "tensor"))
    return jax.shard_map(
        per_device, mesh=mesh, in_specs=in_specs, out_specs=out_specs, check_vma=False
    )
```

```python
import functools
import math

import jax
import jax.numpy as jnp
from jax import lax
from jax.experimental import pallas as pl
from jax.experimental.pallas import tpu as pltpu
from jax.sharding import PartitionSpec as P

ROWS = 28672
COLS = 8192
RANK = 512
F32 = jnp.float32
BF16 = jnp.bfloat16
HIGHEST = lax.Precision.HIGHEST
SHAPE = (4, 8, 4)
VMEM_LIMIT = 56 * 1024 * 1024


def dot(a, b, contract=((1,), (0,)), precision=None):
    return lax.dot_general(
        a, b, (contract, ((), ())), precision=precision, preferred_element_type=F32
    )


def update_kernel(shape, cols_total, mom_hbm, grad_hbm, basis_hbm, orth_ref, r_ref, nb_ref, buf,
                  mom, grad, basis, p_part, p_rx, p_sum, p_t,
                  g_send, g_own, g_core, g_xs, g_xrx, g_zs, g_zrx, g_all,
                  t_send, t_own, t_core, t_xs, t_xrx, t_zs, t_zrx, t_all,
                  m, w, sq_own, sq_rx, in_s, core_s, core_r, x_s, x_r, y_s, y_r, z_s, z_r, xy_s, xy_r):
    nx, nz, ny = shape
    zero, y = lax.axis_index("zero"), lax.axis_index("tensor")
    c = lax.rem(zero, 2)
    z = lax.rem(lax.div(zero, 2), nz)
    x = lax.div(zero, 2 * nz)
    other = 1 - c

    def at(xx, zz, cc):
        return (xx * nz + zz) * 2 + cc

    def hop(axis, d):
        if axis == "x":
            return (at(lax.rem(x + d, nx), z, c), y)
        if axis == "z":
            return (at(x, lax.rem(z + d, nz), c), y)
        if axis == "y":
            return (zero, lax.rem(y + d, ny))
        if axis == "xy":
            return (at(lax.rem(x + d[0], nx), z, c), lax.rem(y + d[1], ny))
        return (at(x, z, other), y)

    def copy(src, dst, send, recv, device):
        return pltpu.make_async_remote_copy(
            src_ref=src, dst_ref=dst, send_sem=send, recv_sem=recv,
            device_id=device, device_id_type=pl.DeviceIdType.MESH)

    def far_first(size):
        return sorted(range(1, size), key=lambda d: -min(d, size - d))

    plane = [(i, j) for i in range(nx) for j in range(ny) if i or j]
    plane.sort(key=lambda d: -(min(d[0], nx - d[0]) + min(d[1], ny - d[1])))
    barrier = pltpu.get_barrier_semaphore()
    peers = [hop("xy", d) for d in plane] + [hop("z", d) for d in range(1, nz)] + [hop("core", 1)]
    for peer in peers:
        pl.semaphore_signal(barrier, inc=1, device_id=peer, device_id_type=pl.DeviceIdType.MESH)

    y_order = far_first(ny) + [0]
    loads = {}
    for n, d in enumerate(y_order):
        u = lax.rem(y + d, ny)
        loads[d] = [
            pltpu.make_async_copy(mom_hbm.at[u], mom.at[d], in_s.at[0, d]),
            pltpu.make_async_copy(grad_hbm.at[u], grad.at[d], in_s.at[1, d]),
        ]
        for go in loads[d]:
            go.start()
        if n == 0:
            load_basis = pltpu.make_async_copy(basis_hbm, basis, in_s.at[2, 0])
            load_basis.start()
    load_basis_wait = [load_basis]

    pending = []

    def partial_rows(d):
        for go in loads[d] + load_basis_wait:
            go.wait()
        load_basis_wait.clear()
        rows = (mom[d].astype(F32) + grad[d].astype(F32)).astype(BF16)
        buf[lax.rem(y + d, ny)] = rows
        return dot(rows, basis[...])

    def start_scatter(axis, n, send, rx, sems):
        me, size = {"x": (x, nx), "y": (y, ny), "z": (z, nz)}[axis]
        copies = []
        for d in far_first(size):
            src = send.at[lax.rem(me + d, size)]
            go = copy(src, rx.at[d - 1], sems[0].at[n, d - 1], sems[1].at[n, d - 1], hop(axis, d))
            go.start()
            copies.append(go)
        return copies

    def start_exchange(axis, n, send, rx, sems):
        size = {"x": nx, "y": ny, "z": nz}[axis]
        copies = []
        for d in far_first(size):
            go = copy(send, rx.at[d - 1], sems[0].at[n, d - 1], sems[1].at[n, d - 1], hop(axis, d))
            go.start()
            copies.append(go)
        return copies

    def arrived(copies):
        for go in copies:
            go.wait_recv()
        pending.extend(copies)

    def start_gather(axis, n, view, sems):
        me, size = {"x": (x, nx), "y": (y, ny), "z": (z, nz)}[axis]
        copies = []
        for d in far_first(size):
            go = copy(view(me), view(me), sems[0].at[n, d - 1], sems[1].at[n, d - 1], hop(axis, d))
            go.start()
            copies.append(go)
        return copies

    def gathered(axis, n, view, copies, sems):
        me, size = {"x": (x, nx), "y": (y, ny), "z": (z, nz)}[axis]
        for d in far_first(size):
            src = lax.rem(me - d + size, size)
            copy(view(src), view(src), sems[0].at[n, d - 1], sems[1].at[n, d - 1], hop(axis, d)).wait_recv()
        pending.extend(copies)

    xs, ys, zs = (x_s, x_r), (y_s, y_r), (z_s, z_r)

    for d in y_order[:-1]:
        p_part[d - 1] = partial_rows(d).astype(BF16)
    pl.semaphore_wait(barrier, len(peers))
    p_go = []
    for d in y_order[:-1]:
        go = copy(p_part.at[d - 1], p_rx.at[d - 1], y_s.at[0, d - 1], y_r.at[0, d - 1], hop("y", d))
        go.start()
        p_go.append(go)
    own = partial_rows(0)
    for d, go in zip(y_order, p_go):
        go.wait_recv()
        own = own + p_rx[d - 1].astype(F32)
    p_sum[y] = own.astype(BF16)
    pending += p_go
    p_go = start_gather("y", 1, lambda i: p_sum.at[i], ys)
    gathered("y", 1, lambda i: p_sum.at[i], p_go, ys)

    rows, rank = buf.shape[0] * buf.shape[1], p_sum.shape[2]
    half = rank // 2
    p_all = p_sum[...].reshape(rows, rank)
    p_t[...] = p_all.T.reshape(2, half, rows)
    gcols = rank // ny

    p_cols = [p_all[:, gcols * i: gcols * (i + 1)] for i in range(ny)]
    p_mine = p_cols[0]
    for i in range(1, ny):
        p_mine = jnp.where(y == i, p_cols[i], p_mine)
    g_send[...] = dot(p_t[other], p_mine).reshape(g_send.shape)
    g_go = copy(g_send, g_core, core_s.at[0], core_r.at[0], hop("core", 1))
    g_go.start()
    g_own[...] = dot(p_t[c], p_mine).reshape(g_own.shape)
    arrived([g_go])
    g_xs[...] = g_own[...] + g_core[...]
    g_x = start_scatter("x", 0, g_xs, g_xrx, xs)

    cb = t_send.shape[3]
    t_shape = (t_send.shape[0], t_send.shape[2], cb)
    for k in range(nz):
        cols = buf[:, :, cb * k: cb * (k + 1)].reshape(rows, cb)
        t_send[:, k] = dot(p_t[other], cols).astype(BF16).reshape(t_shape)
    t_go = []
    for i in range(nx):
        go = copy(t_send.at[i], t_core.at[i], core_s.at[1 + i], core_r.at[1 + i], hop("core", 1))
        go.start()
        t_go.append(go)
    arrived(g_x)
    g_zs[...] = sum((g_xrx[d] for d in range(nx - 1)), g_xs[x])
    g_z = start_exchange("z", 0, g_zs, g_zrx, zs)

    for k in range(nz):
        cols = buf[:, :, cb * k: cb * (k + 1)].reshape(rows, cb)
        t_own[:, k] = dot(p_t[c], cols).reshape(t_shape)
    arrived(t_go)

    def add_core(i, carry):
        total = t_own[i] + t_core[i].astype(F32)
        t_own[i] = total
        t_xs[i] = total.astype(BF16)
        return carry

    lax.fori_loop(0, nx, add_core, 0)
    t_copies = {"x": start_scatter("x", 1, t_xs, t_xrx, xs)}

    arrived(g_z)
    g_all[c, x, y] = sum((g_zrx[d] for d in range(nz - 1)), g_zs[...])
    g_xy = []
    for n, d in enumerate(plane):
        go = copy(g_all.at[c, x, y], g_all.at[c, x, y], xy_s.at[n], xy_r.at[n], hop("xy", d))
        go.start()
        g_xy.append(go)
    for n, d in enumerate(plane):
        part = g_all.at[c, lax.rem(x - d[0] + nx, nx), lax.rem(y - d[1] + ny, ny)]
        copy(part, part, xy_s.at[n], xy_r.at[n], hop("xy", d)).wait_recv()
    pending += g_xy
    g_gc = copy(g_all.at[c], g_all.at[c], core_s.at[nx + 2], core_r.at[nx + 2], hop("core", 1))
    g_gc.start()
    copy(g_all.at[other], g_all.at[other], core_s.at[nx + 2], core_r.at[nx + 2], hop("core", 1)).wait_recv()
    pending += [g_gc]

    def sum_x():
        arrived(t_copies["x"])

        def add_x(k, carry):
            total = t_own[x, k]
            for d in range(nx - 1):
                total = total + t_xrx[d, k].astype(F32)
            t_own[x, k] = total
            t_zs[k] = total.astype(BF16)
            return carry

        lax.fori_loop(0, nz, add_x, 0)
        t_copies["z"] = start_scatter("z", 1, t_zs, t_zrx, zs)

    def sum_z():
        arrived(t_copies["z"])
        t_all[c, x, z] = sum((t_zrx[d].astype(F32) for d in range(nz - 1)), t_own[x, z]).astype(BF16)
        t_copies["gz"] = start_gather("z", 2, lambda i: t_all.at[c, x, i], zs)

    def gather_x():
        gathered("z", 2, lambda i: t_all.at[c, x, i], t_copies["gz"], zs)
        t_copies["gx"] = start_gather("x", 2, lambda i: t_all.at[c, i], xs)

    def gather_core():
        gathered("x", 2, lambda i: t_all.at[c, i], t_copies["gx"], xs)
        go = copy(t_all.at[c], t_all.at[c], core_s.at[nx + 1], core_r.at[nx + 1], hop("core", 1))
        go.start()
        copy(t_all.at[other], t_all.at[other], core_s.at[nx + 1], core_r.at[nx + 1], hop("core", 1)).wait_recv()
        pending.append(go)

    nb = rank // 128
    gr = g_all.shape[3] * g_all.shape[4]
    for i in range(2):
        for j in range(nx):
            for k in range(ny):
                lo = (i * nx + j) * gr
                m[lo:lo + gr, gcols * k:gcols * (k + 1)] = g_all[i, j, k].reshape(gr, gcols)
    row = lax.broadcasted_iota(jnp.int32, (128, 128), 0)
    col = lax.broadcasted_iota(jnp.int32, (128, 128), 1)
    eye = jnp.where(row == col, 1.0, 0.0)
    for i in range(nb):
        for j in range(nb):
            m[128 * i:128 * (i + 1), rank + 128 * j:rank + 128 * (j + 1)] = eye if i == j else jnp.zeros_like(eye)
    steps = 16 * nb
    plan = {2 * steps // 64: sum_x, 22 * steps // 64: sum_z, 42 * steps // 64: gather_x}
    for k in range(nb):
        lo, hi = 128 * k, 128 * (k + 1)
        w[:, 0:128] = m[lo:hi, lo:hi]
        w[:, 128:256] = eye
        factor128(w, {n - 16 * k: f for n, f in plan.items()})
        inv = w[:, 128:256]
        m[lo:hi, hi:rank + hi] = dot(inv, m[lo:hi, hi:rank + hi], precision=HIGHEST)
        if k + 1 < nb:
            m[hi:, hi:rank + hi] = m[hi:, hi:rank + hi] - dot(
                m[lo:hi, hi:rank], m[lo:hi, hi:rank + hi], ((0,), (0,)), HIGHEST)
    high, low = split(m[:, rank:])
    orth_ref[...] = (dot(p_all, high, ((1,), (1,))) + dot(p_all, low, ((1,), (1,)))).astype(BF16)
    gather_core()

    ones = jnp.ones((8, cb), F32)
    total = jnp.zeros((8, rank), F32)
    for k in range(nz):
        t = t_all[:, :, k].reshape(rank, cb)
        r = dot(high, t) + dot(low, t)
        r_ref[:, cb * k:cb * (k + 1)] = r.astype(BF16)
        nb_ref[:, cb * k:cb * (k + 1)] = r.astype(F32)
        total = total + dot(ones, r * r, ((1,), (1,)), HIGHEST)
    sq_own[...] = total
    sq_go = start_exchange("y", 2, sq_own, sq_rx, ys)
    arrived(sq_go)
    total = sum((sq_rx[d] for d in range(ny - 1)), sq_own[...])
    scale = lax.rsqrt(total / cols_total + 1e-06)
    scale = dot(scale, jnp.full((8, 128), 0.125, F32), ((0,), (0,)), HIGHEST)
    for k in range(nz * cb // 128):
        nb_ref[:, 128 * k:128 * (k + 1)] = nb_ref[:, 128 * k:128 * (k + 1)] * scale
    for go in pending:
        go.wait_send()


def update_call(shape, cols_total, mom, grad, basis):
    nx, nz, ny = shape
    rows, cols = mom.shape
    rank = basis.shape[1]
    part, cb, rb, gb = rows // ny, cols // nz, rank // (2 * nx), rank // (2 * nx * nz)
    gc = rank // ny
    vmem, sem = pltpu.VMEM, pltpu.SemaphoreType.DMA
    space = pl.BlockSpec(memory_space=pltpu.VMEM)
    hbm = pl.BlockSpec(memory_space=pl.ANY)
    return pl.pallas_call(
        functools.partial(update_kernel, shape, cols_total),
        out_shape=(
            jax.ShapeDtypeStruct((rows, rank), BF16),
            jax.ShapeDtypeStruct((rank, cols), BF16),
            jax.ShapeDtypeStruct((rank, cols), F32),
            jax.ShapeDtypeStruct((ny, part, cols), BF16),
        ),
        in_specs=[hbm] * 3,
        out_specs=(space,) * 4,
        scratch_shapes=[
            vmem((ny, part, cols), BF16),
            vmem((ny, part, cols), BF16),
            vmem((cols, rank), BF16),
            vmem((ny - 1, part, rank), BF16),
            vmem((ny - 1, part, rank), BF16),
            vmem((ny, part, rank), BF16),
            vmem((2, rank // 2, rows), BF16),
            vmem((nx, nz, gb, gc), F32),
            vmem((nx, nz, gb, gc), F32),
            vmem((nx, nz, gb, gc), F32),
            vmem((nx, nz, gb, gc), F32),
            vmem((nx - 1, nz, gb, gc), F32),
            vmem((nz, gb, gc), F32),
            vmem((nz - 1, nz, gb, gc), F32),
            vmem((2, nx, ny, nz, gb, gc), F32),
            vmem((nx, nz, rb, cb), BF16),
            vmem((nx, nz, rb, cb), F32),
            vmem((nx, nz, rb, cb), BF16),
            vmem((nx, nz, rb, cb), BF16),
            vmem((nx - 1, nz, rb, cb), BF16),
            vmem((nz, rb, cb), BF16),
            vmem((nz - 1, rb, cb), BF16),
            vmem((2, nx, nz, rb, cb), BF16),
            vmem((rank, 2 * rank), F32),
            vmem((128, 256), F32),
            vmem((8, rank), F32),
            vmem((ny - 1, 8, rank), F32),
            sem((3, ny)),
            sem((nx + 3,)), sem((nx + 3,)),
            sem((3, nx - 1)), sem((3, nx - 1)),
            sem((3, ny - 1)), sem((3, ny - 1)),
            sem((3, nz - 1)), sem((3, nz - 1)),
            sem((nx * ny - 1,)), sem((nx * ny - 1,)),
        ],
        compiler_params=pltpu.CompilerParams(
            collective_id=0, has_side_effects=True, vmem_limit_bytes=VMEM_LIMIT),
        name="update",
    )(mom.reshape(ny, part, cols), grad.reshape(ny, part, cols), basis)


def factor8(cols):
    e = [[jnp.broadcast_to(cols[k][q:q + 1, :], (8, 128)) for k in range(q + 1)] for q in range(8)]
    low = [[None] * 8 for _ in range(8)]
    inv = [[None] * 8 for _ in range(8)]
    for p in range(8):
        inv[p][p] = lax.rsqrt(e[p][p])
        for q in range(p + 1, 8):
            low[q][p] = e[q][p] * inv[p][p]
        for q in range(p + 1, 8):
            for k in range(p + 1, q + 1):
                e[q][k] = e[q][k] - low[q][p] * low[k][p]
    for q in range(8):
        for k in range(q):
            acc = low[q][k] * inv[k][k]
            for m in range(k + 1, q):
                acc = acc + low[q][m] * inv[m][k]
            inv[q][k] = -acc * inv[q][q]
    return inv


def lanes(x, k):
    return jnp.broadcast_to(x[:, k:k + 1], (8, 128))


def rows8(x, k):
    return jnp.broadcast_to(x[k:k + 1, :], (8, 128))


def factor128(r, between):
    sub = lax.broadcasted_iota(jnp.int32, (8, 128), 0)
    for s in range(16):
        if s in between:
            between[s]()
        lo = 8 * s
        a, v = r[lo:lo + 8, 0:128], r[lo:lo + 8, 128:256]
        cols = [lanes(a, lo + k) for k in range(8)]
        if s < 15:
            an, vn = r[lo + 8:lo + 16, 0:128], r[lo + 8:lo + 16, 128:256]
            nxt = [lanes(an, lo + k) for k in range(8)]
        inv = factor8(cols)
        new_a = new_v = None
        for k in range(8):
            m = jnp.where(sub == k, inv[k][k], 0.0)
            for q in range(k + 1, 8):
                m = jnp.where(sub == q, inv[q][k], m)
            ta, tv = m * rows8(a, k), m * rows8(v, k)
            new_a = ta if new_a is None else new_a + ta
            new_v = tv if new_v is None else new_v + tv
        r[lo:lo + 8, 128:256] = new_v
        if s < 15:
            for k in range(8):
                lc = nxt[0] * inv[k][0]
                for j in range(1, k + 1):
                    lc = lc + nxt[j] * inv[k][j]
                an = an - lc * rows8(new_a, k)
                vn = vn - lc * rows8(new_v, k)
            r[lo + 8:lo + 16, 0:128], r[lo + 8:lo + 16, 128:256] = an, vn
        if s < 14:
            both = jnp.concatenate([new_a, new_v], axis=1)
            update = dot(new_a, both, ((0,), (0,)), HIGHEST)
            r[lo + 16:128, :] = r[lo + 16:128, :] - update[lo + 16:128, :]


def split(x):
    high = x.astype(BF16)
    return high, (x - high.astype(F32)).astype(BF16)


def outputs_kernel(orth, buf, r_t, nb_t, mom_out, basis_out, dir_out):
    factor = orth[...]
    low_rank = dot(factor, r_t[...])
    mom_out[...] = (buf[...].astype(F32) - 0.05 * low_rank).astype(BF16)
    new_basis = nb_t[...].astype(BF16)
    dir_out[...] = (math.sqrt(ROWS / RANK) * dot(factor, new_basis)).astype(BF16)
    basis_out[...] = new_basis.T


def outputs_call(orth, buf, r_t, nb_t):
    rows, cols = buf.shape
    rank = orth.shape[1]
    wide = 256
    block = lambda shape, place: pl.BlockSpec(shape, place)
    return pl.pallas_call(
        outputs_kernel,
        grid=(cols // wide,),
        out_shape=(
            jax.ShapeDtypeStruct((rows, cols), BF16),
            jax.ShapeDtypeStruct((cols, rank), BF16),
            jax.ShapeDtypeStruct((rows, cols), BF16),
        ),
        in_specs=[
            block((rows, rank), lambda i: (0, 0)),
            block((rows, wide), lambda i: (0, i)),
            block((rank, wide), lambda i: (0, i)),
            block((rank, wide), lambda i: (0, i)),
        ],
        out_specs=(
            block((rows, wide), lambda i: (0, i)),
            block((wide, rank), lambda i: (i, 0)),
            block((rows, wide), lambda i: (0, i)),
        ),
        compiler_params=pltpu.CompilerParams(vmem_limit_bytes=VMEM_LIMIT),
        name="outputs",
    )(orth, buf, r_t, nb_t)


def per_device(momentum, gradient, old_basis):
    orth, r_t, nb_t, buf = update_call(SHAPE, COLS, momentum, gradient, old_basis)
    return outputs_call(orth, buf.reshape(momentum.shape), r_t, nb_t)


def solution(mesh):
    in_specs = (P("zero", "tensor"), P("zero", "tensor"), P("tensor", None))
    out_specs = (P("zero", "tensor"), P("tensor", None), P("zero", "tensor"))
    return jax.shard_map(
        per_device, mesh=mesh, in_specs=in_specs, out_specs=out_specs, check_vma=False
    )
```

```python
import functools
import math

import jax
import jax.numpy as jnp
from jax import lax
from jax.experimental import pallas as pl
from jax.experimental.pallas import tpu as pltpu
from jax.sharding import PartitionSpec as P

ROWS = 28672
COLS = 8192
RANK = 512
F32 = jnp.float32
BF16 = jnp.bfloat16
HIGHEST = lax.Precision.HIGHEST
SHAPE = (4, 8, 4)
VMEM_LIMIT = 40 * 1024 * 1024
PIECES = 4


def dot(a, b, contract=((1,), (0,)), precision=None):
    return lax.dot_general(
        a, b, (contract, ((), ())), precision=precision, preferred_element_type=F32
    )


def update_kernel(shape, cols_total, mom_hbm, grad_hbm, basis_hbm, orth_ref, r_ref, nb_ref, buf,
                  mom, grad, basis, p_part, p_rx, p_sum, p_t,
                  g_send, g_own, g_core, g_xs, g_xrx, g_zs, g_zrx, g_all,
                  t_send, t_own, t_core, t_xs, t_xrx, t_zf, t_zs, t_zrx, t_all,
                  r_f32, m, w, sq_own, sq_rx, in_s, core_s, core_r, x_s, x_r, y_s, y_r, z_s, z_r, xy_s, xy_r):
    nx, nz, ny = shape
    zero, y = lax.axis_index("zero"), lax.axis_index("tensor")
    c = lax.rem(zero, 2)
    z = lax.rem(lax.div(zero, 2), nz)
    x = lax.div(zero, 2 * nz)
    other = 1 - c

    def at(xx, zz, cc):
        return (xx * nz + zz) * 2 + cc

    def hop(axis, d):
        if axis == "x":
            return (at(lax.rem(x + d, nx), z, c), y)
        if axis == "z":
            return (at(x, lax.rem(z + d, nz), c), y)
        if axis == "y":
            return (zero, lax.rem(y + d, ny))
        if axis == "xy":
            return (at(lax.rem(x + d[0], nx), z, c), lax.rem(y + d[1], ny))
        return (at(x, z, other), y)

    def copy(src, dst, send, recv, device):
        return pltpu.make_async_remote_copy(
            src_ref=src, dst_ref=dst, send_sem=send, recv_sem=recv,
            device_id=device, device_id_type=pl.DeviceIdType.MESH)

    def far_first(size):
        return sorted(range(1, size), key=lambda d: -min(d, size - d))

    plane = [(i, j) for i in range(nx) for j in range(ny) if i or j]
    plane.sort(key=lambda d: -(min(d[0], nx - d[0]) + min(d[1], ny - d[1])))
    barrier = pltpu.get_barrier_semaphore()
    peers = [hop("xy", d) for d in plane] + [hop("z", d) for d in range(1, nz)] + [hop("core", 1)]
    for peer in peers:
        pl.semaphore_signal(barrier, inc=1, device_id=peer, device_id_type=pl.DeviceIdType.MESH)

    y_order = far_first(ny) + [0]
    loads = {}
    for n, d in enumerate(y_order):
        u = lax.rem(y + d, ny)
        loads[d] = [
            pltpu.make_async_copy(mom_hbm.at[u], mom.at[d], in_s.at[0, d]),
            pltpu.make_async_copy(grad_hbm.at[u], grad.at[d], in_s.at[1, d]),
        ]
        for go in loads[d]:
            go.start()
        if n == 0:
            load_basis = pltpu.make_async_copy(basis_hbm, basis, in_s.at[2, 0])
            load_basis.start()
    load_basis_wait = [load_basis]

    pending = []

    def partial_rows(d):
        for go in loads[d] + load_basis_wait:
            go.wait()
        load_basis_wait.clear()
        rows = (mom[d].astype(F32) + grad[d].astype(F32)).astype(BF16)
        buf[lax.rem(y + d, ny)] = rows
        return dot(rows, basis[...])

    def start_scatter(axis, n, send, rx, sems):
        me, size = {"x": (x, nx), "y": (y, ny), "z": (z, nz)}[axis]
        copies = []
        for d in far_first(size):
            src = send.at[lax.rem(me + d, size)]
            go = copy(src, rx.at[d - 1], sems[0].at[n, d - 1], sems[1].at[n, d - 1], hop(axis, d))
            go.start()
            copies.append(go)
        return copies

    def start_exchange(axis, n, send, rx, sems):
        size = {"x": nx, "y": ny, "z": nz}[axis]
        copies = []
        for d in far_first(size):
            go = copy(send, rx.at[d - 1], sems[0].at[n, d - 1], sems[1].at[n, d - 1], hop(axis, d))
            go.start()
            copies.append(go)
        return copies

    def arrived(copies):
        for go in copies:
            go.wait_recv()
        pending.extend(copies)

    def start_gather(axis, n, view, sems):
        me, size = {"x": (x, nx), "y": (y, ny), "z": (z, nz)}[axis]
        copies = []
        for d in far_first(size):
            go = copy(view(me), view(me), sems[0].at[n, d - 1], sems[1].at[n, d - 1], hop(axis, d))
            go.start()
            copies.append(go)
        return copies

    def gathered(axis, n, view, copies, sems):
        me, size = {"x": (x, nx), "y": (y, ny), "z": (z, nz)}[axis]
        for d in far_first(size):
            src = lax.rem(me - d + size, size)
            copy(view(src), view(src), sems[0].at[n, d - 1], sems[1].at[n, d - 1], hop(axis, d)).wait_recv()
        pending.extend(copies)

    xs, ys, zs = (x_s, x_r), (y_s, y_r), (z_s, z_r)

    for d in y_order[:-1]:
        p_part[d - 1] = partial_rows(d).astype(BF16)
    pl.semaphore_wait(barrier, len(peers))
    rank = p_sum.shape[2]
    sides = [pl.ds(0, rank // 2), pl.ds(rank // 2, rank // 2)]
    p_go = []
    for n, side in enumerate(sides):
        p_go.append([])
        for d in y_order[:-1]:
            go = copy(p_part.at[d - 1, :, side], p_rx.at[d - 1, :, side],
                      y_s.at[n, d - 1], y_r.at[n, d - 1], hop("y", d))
            go.start()
            p_go[n].append(go)
    own = partial_rows(0)
    p_gather = []
    for n, side in enumerate(sides):
        arrived(p_go[n])
        total = own[:, n * rank // 2:(n + 1) * rank // 2]
        for d in y_order[:-1]:
            total = total + p_rx[d - 1, :, side].astype(F32)
        p_sum[y, :, side] = total.astype(BF16)
        p_gather.append(start_gather("y", 2 + n, lambda i: p_sum.at[i, :, side], ys))
    for n, side in enumerate(sides):
        gathered("y", 2 + n, lambda i: p_sum.at[i, :, side], p_gather[n], ys)

    rows = buf.shape[0] * buf.shape[1]
    half = rank // 2
    p_all = p_sum[...].reshape(rows, rank)
    p_t[...] = p_all.T.reshape(2, half, rows)
    gcols = rank // ny

    p_cols = [p_all[:, gcols * i: gcols * (i + 1)] for i in range(ny)]
    p_mine = p_cols[0]
    for i in range(1, ny):
        p_mine = jnp.where(y == i, p_cols[i], p_mine)
    g_send[...] = dot(p_t[other], p_mine).reshape(g_send.shape)
    g_go = copy(g_send, g_core, core_s.at[0], core_r.at[0], hop("core", 1))
    g_go.start()
    g_own[...] = dot(p_t[c], p_mine).reshape(g_own.shape)
    arrived([g_go])
    g_xs[...] = g_own[...] + g_core[...]
    g_x = start_scatter("x", 0, g_xs, g_xrx, xs)

    pieces, _, _, tr, cb = t_send.shape
    t_shape = (pieces, nx, tr, cb)
    for k in range(nz):
        cols = buf[:, :, cb * k: cb * (k + 1)].reshape(rows, cb)
        t_send[:, :, k] = dot(p_t[other], cols).astype(BF16).reshape(t_shape)
    t_core_go = []
    for p in range(pieces):
        go = copy(t_send.at[p], t_core.at[p], core_s.at[2 + p], core_r.at[2 + p], hop("core", 1))
        go.start()
        t_core_go.append(go)
    for k in range(nz):
        cols = buf[:, :, cb * k: cb * (k + 1)].reshape(rows, cb)
        t_own[:, :, k] = dot(p_t[c], cols).reshape(t_shape)

    t_go = {}

    def sum_core(p):
        arrived([t_core_go[p]])
        total = t_own[p] + t_core[p].astype(F32)
        t_own[p] = total
        t_xs[p] = total.astype(BF16)
        t_go["x", p] = start_scatter("x", 1 + p, t_xs.at[p], t_xrx.at[p], xs)

    def sum_x(p):
        arrived(t_go["x", p])
        total = t_own[p, x]
        for d in range(nx - 1):
            total = total + t_xrx[p, d].astype(F32)
        t_zf[p] = total
        t_zs[p] = total.astype(BF16)
        t_go["z", p] = start_scatter("z", 1 + p, t_zs.at[p], t_zrx.at[p], zs)

    def sum_z(p):
        arrived(t_go["z", p])
        total = t_zf[p, z]
        for d in range(nz - 1):
            total = total + t_zrx[p, d].astype(F32)
        t_all[c, p, x, z] = total.astype(BF16)
        t_go["gz", p] = start_gather("z", 1 + pieces + p, lambda i: t_all.at[c, p, x, i], zs)

    def gather_x(p):
        gathered("z", 1 + pieces + p, lambda i: t_all.at[c, p, x, i], t_go["gz", p], zs)
        t_go["gx", p] = start_gather("x", 1 + pieces + p, lambda i: t_all.at[c, p, i], xs)

    def gather_core(p):
        gathered("x", 1 + pieces + p, lambda i: t_all.at[c, p, i], t_go["gx", p], xs)
        t_go["gc", p] = copy(t_all.at[c, p], t_all.at[c, p], core_s.at[2 + pieces + p],
                             core_r.at[2 + pieces + p], hop("core", 1))
        t_go["gc", p].start()

    def got_core(p):
        part = t_all.at[other, p]
        copy(part, part, core_s.at[2 + pieces + p], core_r.at[2 + pieces + p], hop("core", 1)).wait_recv()
        pending.append(t_go["gc", p])

    arrived(g_x)
    g_zs[...] = sum((g_xrx[d] for d in range(nx - 1)), g_xs[x])
    g_z = start_exchange("z", 0, g_zs, g_zrx, zs)
    for p in range(pieces):
        sum_core(p)
    for p in range(pieces // 2):
        sum_x(p)

    arrived(g_z)
    g_all[c, x, y] = sum((g_zrx[d] for d in range(nz - 1)), g_zs[...])
    g_xy = []
    for n, d in enumerate(plane):
        go = copy(g_all.at[c, x, y], g_all.at[c, x, y], xy_s.at[n], xy_r.at[n], hop("xy", d))
        go.start()
        g_xy.append(go)
    for p in range(pieces // 2, pieces):
        sum_x(p)
    for p in range(pieces // 2):
        sum_z(p)
    for n, d in enumerate(plane):
        part = g_all.at[c, lax.rem(x - d[0] + nx, nx), lax.rem(y - d[1] + ny, ny)]
        copy(part, part, xy_s.at[n], xy_r.at[n], hop("xy", d)).wait_recv()
    pending += g_xy
    g_gc = copy(g_all.at[c], g_all.at[c], core_s.at[1], core_r.at[1], hop("core", 1))
    g_gc.start()
    for p in range(pieces // 2, pieces):
        sum_z(p)
    copy(g_all.at[other], g_all.at[other], core_s.at[1], core_r.at[1], hop("core", 1)).wait_recv()
    pending += [g_gc]

    nb = rank // 128
    gr = g_all.shape[3] * g_all.shape[4]
    for i in range(2):
        for j in range(nx):
            for k in range(ny):
                lo = (i * nx + j) * gr
                m[lo:lo + gr, gcols * k:gcols * (k + 1)] = g_all[i, j, k].reshape(gr, gcols)
    row = lax.broadcasted_iota(jnp.int32, (128, 128), 0)
    col = lax.broadcasted_iota(jnp.int32, (128, 128), 1)
    eye = jnp.where(row == col, 1.0, 0.0)
    for i in range(nb):
        for j in range(nb):
            m[128 * i:128 * (i + 1), rank + 128 * j:rank + 128 * (j + 1)] = eye if i == j else jnp.zeros_like(eye)
    stages = [(gather_x, p) for p in range(pieces)] + [(gather_core, p) for p in range(pieces)]
    first = (2, 4, 12, 20, 36, 44, 52, 60)
    plan = {at_step * nb // 4: stage for at_step, stage in zip(first, stages)}
    assert len(plan) == len(stages)
    for k in range(nb):
        lo, hi = 128 * k, 128 * (k + 1)
        w[:, 0:128] = m[lo:hi, lo:hi]
        w[:, 128:256] = eye
        factor128(w, {n - 16 * k: f for n, f in plan.items()})
        inv = w[:, 128:256]
        m[lo:hi, hi:rank + hi] = dot(inv, m[lo:hi, hi:rank + hi], precision=HIGHEST)
        if k + 1 < nb:
            m[hi:, hi:rank + hi] = m[hi:, hi:rank + hi] - dot(
                m[lo:hi, hi:rank], m[lo:hi, hi:rank + hi], ((0,), (0,)), HIGHEST)
    high, low = split(m[:, rank:])
    orth_ref[...] = (dot(p_all, high, ((1,), (1,))) + dot(p_all, low, ((1,), (1,)))).astype(BF16)
    for p in range(pieces):
        got_core(p)

    ones = jnp.ones((8, cb), F32)
    total = jnp.zeros((8, rank), F32)
    for k in range(nz):
        t = t_all[:, :, :, k].reshape(rank, cb)
        r = dot(high, t) + dot(low, t)
        r_ref[:, cb * k:cb * (k + 1)] = r.astype(BF16)
        r_f32[:, cb * k:cb * (k + 1)] = r
        total = total + dot(ones, r * r, ((1,), (1,)), HIGHEST)
    sq_own[...] = total
    sq_go = start_exchange("y", 4, sq_own, sq_rx, ys)
    arrived(sq_go)
    total = sum((sq_rx[d] for d in range(ny - 1)), sq_own[...])
    scale = lax.rsqrt(total / cols_total + 1e-06)
    scale = dot(scale, jnp.full((8, 128), 0.125, F32), ((0,), (0,)), HIGHEST)
    for k in range(nz * cb // 128):
        part = pl.ds(128 * k, 128)
        nb_ref[:, part] = (r_f32[:, part] * scale).astype(BF16)
    for go in pending:
        go.wait_send()


def update_call(shape, cols_total, mom, grad, basis):
    nx, nz, ny = shape
    rows, cols = mom.shape
    rank = basis.shape[1]
    part, cb, gb = rows // ny, cols // nz, rank // (2 * nx * nz)
    gc, np = rank // ny, PIECES
    tr = rank // (2 * np * nx)
    args = (mom.reshape(ny, part, cols), grad.reshape(ny, part, cols), basis)
    vmem, sem = pltpu.VMEM, pltpu.SemaphoreType.DMA
    space = pl.BlockSpec(memory_space=pltpu.VMEM)
    hbm = pl.BlockSpec(memory_space=pltpu.MemorySpace.HBM)
    return pl.pallas_call(
        functools.partial(update_kernel, shape, cols_total),
        out_shape=(
            vmem((rows, rank), BF16),
            vmem((rank, cols), BF16),
            vmem((rank, cols), BF16),
            vmem((ny, part, cols), BF16),
        ),
        in_specs=[hbm] * 3,
        out_specs=(space,) * 4,
        scratch_shapes=[
            vmem((ny, part, cols), BF16),
            vmem((ny, part, cols), BF16),
            vmem((cols, rank), BF16),
            vmem((ny - 1, part, rank), BF16),
            vmem((ny - 1, part, rank), BF16),
            vmem((ny, part, rank), BF16),
            vmem((2, rank // 2, rows), BF16),
            vmem((nx, nz, gb, gc), F32),
            vmem((nx, nz, gb, gc), F32),
            vmem((nx, nz, gb, gc), F32),
            vmem((nx, nz, gb, gc), F32),
            vmem((nx - 1, nz, gb, gc), F32),
            vmem((nz, gb, gc), F32),
            vmem((nz - 1, nz, gb, gc), F32),
            vmem((2, nx, ny, nz, gb, gc), F32),
            vmem((np, nx, nz, tr, cb), BF16),
            vmem((np, nx, nz, tr, cb), F32),
            vmem((np, nx, nz, tr, cb), BF16),
            vmem((np, nx, nz, tr, cb), BF16),
            vmem((np, nx - 1, nz, tr, cb), BF16),
            vmem((np, nz, tr, cb), F32),
            vmem((np, nz, tr, cb), BF16),
            vmem((np, nz - 1, tr, cb), BF16),
            vmem((2, np, nx, nz, tr, cb), BF16),
            vmem((rank, cols), F32),
            vmem((rank, 2 * rank), F32),
            vmem((128, 256), F32),
            vmem((8, rank), F32),
            vmem((ny - 1, 8, rank), F32),
            sem((3, ny)),
            sem((2 + 2 * np,)), sem((2 + 2 * np,)),
            sem((1 + 2 * np, nx - 1)), sem((1 + 2 * np, nx - 1)),
            sem((5, ny - 1)), sem((5, ny - 1)),
            sem((1 + 2 * np, nz - 1)), sem((1 + 2 * np, nz - 1)),
            sem((nx * ny - 1,)), sem((nx * ny - 1,)),
        ],
        compiler_params=pltpu.CompilerParams(
            collective_id=0, has_side_effects=True, vmem_limit_bytes=VMEM_LIMIT),
        name="update",
    )(*(pltpu.with_memory_space_constraint(v, pltpu.MemorySpace.HBM) for v in args))


def factor8(cols):
    e = [[jnp.broadcast_to(cols[k][q:q + 1, :], (8, 128)) for k in range(q + 1)] for q in range(8)]
    low = [[None] * 8 for _ in range(8)]
    inv = [[None] * 8 for _ in range(8)]
    for p in range(8):
        inv[p][p] = lax.rsqrt(e[p][p])
        for q in range(p + 1, 8):
            low[q][p] = e[q][p] * inv[p][p]
        for q in range(p + 1, 8):
            for k in range(p + 1, q + 1):
                e[q][k] = e[q][k] - low[q][p] * low[k][p]
    for q in range(8):
        for k in range(q):
            acc = low[q][k] * inv[k][k]
            for m in range(k + 1, q):
                acc = acc + low[q][m] * inv[m][k]
            inv[q][k] = -acc * inv[q][q]
    return inv


def lanes(x, k):
    return jnp.broadcast_to(x[:, k:k + 1], (8, 128))


def rows8(x, k):
    return jnp.broadcast_to(x[k:k + 1, :], (8, 128))


def split3(x):
    high = x.astype(BF16).astype(F32)
    x = x - high
    mid = x.astype(BF16).astype(F32)
    return high, mid, x - mid


def rank8(a, v):
    ha, ma, la = split3(a)
    hv, mv, lv = split3(v)
    left = jnp.concatenate([ha, ma, la, ha, ma, ha], axis=0).astype(BF16)
    right_a = jnp.concatenate([ha, ha, ha, ma, ma, la], axis=0)
    right_v = jnp.concatenate([hv, hv, hv, mv, mv, lv], axis=0)
    return dot(left, jnp.concatenate([right_a, right_v], axis=1).astype(BF16), ((0,), (0,)))


def factor128(r, between):
    sub = lax.broadcasted_iota(jnp.int32, (8, 128), 0)
    a, v = r[0:8, 0:128], r[0:8, 128:256]
    cols = [lanes(a, k) for k in range(8)]
    for s in range(16):
        if s in between:
            between[s][0](between[s][1])
        lo = 8 * s
        if s < 15:
            an, vn = r[lo + 8:lo + 16, 0:128], r[lo + 8:lo + 16, 128:256]
            below = [lanes(an, lo + k) for k in range(8)]
            ahead = [lanes(an, lo + 8 + k) for k in range(8)]
        inv = factor8(cols)
        new_a = new_v = None
        for k in range(8):
            m = jnp.where(sub == k, inv[k][k], 0.0)
            for q in range(k + 1, 8):
                m = jnp.where(sub == q, inv[q][k], m)
            ta, tv = m * rows8(a, k), m * rows8(v, k)
            new_a = ta if new_a is None else new_a + ta
            new_v = tv if new_v is None else new_v + tv
        r[lo:lo + 8, 128:256] = new_v
        if s < 15:
            low = []
            for k in range(8):
                acc = below[0] * inv[k][0]
                for j in range(1, k + 1):
                    acc = acc + below[j] * inv[k][j]
                low.append(acc)
            cols = []
            for k in range(8):
                an = an - low[k] * rows8(new_a, k)
                vn = vn - low[k] * rows8(new_v, k)
                acc = ahead[k]
                for j in range(8):
                    acc = acc - low[j] * rows8(low[j], k)
                cols.append(acc)
            a, v = an, vn
        if s < 14:
            r[lo + 16:128, :] = r[lo + 16:128, :] - rank8(new_a, new_v)[lo + 16:128, :]


def split(x):
    high = x.astype(BF16)
    return high, (x - high.astype(F32)).astype(BF16)


def outputs_kernel(orth, buf, r_t, nb_t, mom_hbm, basis_hbm, dir_hbm, mom_out, basis_out, dir_out, sems):
    blocks, rows, wide = mom_out.shape
    factor = orth[...]
    copies = []
    for i in range(blocks):
        place = pl.ds(i * wide, wide)
        low_rank = dot(factor, r_t[:, place])
        mine = buf[:, :, place].reshape(rows, wide)
        mom_out[i] = (mine.astype(F32) - 0.05 * low_rank).astype(BF16)
        new_basis = nb_t[:, place]
        basis_out[place, :] = new_basis.T
        dir_out[i] = (math.sqrt(ROWS / RANK) * dot(factor, new_basis)).astype(BF16)
        for n, (src, dst) in enumerate((
            (mom_out.at[i], mom_hbm.at[:, place]),
            (basis_out.at[place, :], basis_hbm.at[place, :]),
            (dir_out.at[i], dir_hbm.at[:, place]),
        )):
            go = pltpu.make_async_copy(src, dst, sems.at[n, i])
            go.start()
            copies.append(go)
    for go in copies:
        go.wait()


def outputs_call(orth, buf, r_t, nb_t):
    rows, cols = buf.shape[0] * buf.shape[1], buf.shape[2]
    rank = orth.shape[1]
    wide = 256
    blocks = cols // wide
    space = pl.BlockSpec(memory_space=pltpu.VMEM)
    hbm = pl.BlockSpec(memory_space=pl.ANY)
    args = [pltpu.with_memory_space_constraint(v, pltpu.VMEM) for v in (orth, buf, r_t, nb_t)]
    return pl.pallas_call(
        outputs_kernel,
        out_shape=(
            jax.ShapeDtypeStruct((rows, cols), BF16),
            jax.ShapeDtypeStruct((cols, rank), BF16),
            jax.ShapeDtypeStruct((rows, cols), BF16),
        ),
        in_specs=[space] * 4,
        out_specs=(hbm,) * 3,
        scratch_shapes=[
            pltpu.VMEM((blocks, rows, wide), BF16),
            pltpu.VMEM((cols, rank), BF16),
            pltpu.VMEM((blocks, rows, wide), BF16),
            pltpu.SemaphoreType.DMA((3, blocks)),
        ],
        compiler_params=pltpu.CompilerParams(vmem_limit_bytes=VMEM_LIMIT),
        name="outputs",
    )(*args)


def per_device(momentum, gradient, old_basis):
    orth, r_t, nb_t, buf = update_call(SHAPE, COLS, momentum, gradient, old_basis)
    return outputs_call(orth, buf, r_t, nb_t)


def solution(mesh):
    in_specs = (P("zero", "tensor"), P("zero", "tensor"), P("tensor", None))
    out_specs = (P("zero", "tensor"), P("tensor", None), P("zero", "tensor"))
    return jax.shard_map(
        per_device, mesh=mesh, in_specs=in_specs, out_specs=out_specs, check_vma=False
    )
```

```python
import functools
import math

import jax
import jax.numpy as jnp
from jax import lax
from jax.experimental import pallas as pl
from jax.experimental.pallas import tpu as pltpu
from jax.sharding import PartitionSpec as P

ROWS = 28672
COLS = 8192
RANK = 512
F32 = jnp.float32
BF16 = jnp.bfloat16
HIGHEST = lax.Precision.HIGHEST
SHAPE = (4, 8, 4)
VMEM_LIMIT = 40 * 1024 * 1024
PIECES = 4


def dot(a, b, contract=((1,), (0,)), precision=None):
    return lax.dot_general(
        a, b, (contract, ((), ())), precision=precision, preferred_element_type=F32
    )


def update_kernel(shape, cols_total, mom_hbm, grad_hbm, basis_hbm, orth_ref, mom_ref, nb_ref,
                  buf, mom, grad, basis, p_part, p_rx, p_sum, p_t,
                  g_send, g_own, g_core, g_xs, g_xrx, g_zs, g_zrx, g_all,
                  t_send, t_own, t_core, t_xs, t_xrx, t_zf, t_zs, t_zrx, t_all,
                  r_f32, m, w, sq_own, sq_rx, in_s, core_s, core_r, x_s, x_r, y_s, y_r, z_s, z_r, xy_s, xy_r):
    nx, nz, ny = shape
    zero, y = lax.axis_index("zero"), lax.axis_index("tensor")
    c = lax.rem(zero, 2)
    z = lax.rem(lax.div(zero, 2), nz)
    x = lax.div(zero, 2 * nz)
    other = 1 - c

    def at(xx, zz, cc):
        return (xx * nz + zz) * 2 + cc

    def hop(axis, d):
        if axis == "x":
            return (at(lax.rem(x + d, nx), z, c), y)
        if axis == "z":
            return (at(x, lax.rem(z + d, nz), c), y)
        if axis == "y":
            return (zero, lax.rem(y + d, ny))
        if axis == "xy":
            return (at(lax.rem(x + d[0], nx), z, c), lax.rem(y + d[1], ny))
        return (at(x, z, other), y)

    def copy(src, dst, send, recv, device):
        return pltpu.make_async_remote_copy(
            src_ref=src, dst_ref=dst, send_sem=send, recv_sem=recv,
            device_id=device, device_id_type=pl.DeviceIdType.MESH)

    def far_first(size):
        return sorted(range(1, size), key=lambda d: -min(d, size - d))

    plane = [(i, j) for i in range(nx) for j in range(ny) if i or j]
    plane.sort(key=lambda d: -(min(d[0], nx - d[0]) + min(d[1], ny - d[1])))
    barrier = pltpu.get_barrier_semaphore()
    peers = [hop("xy", d) for d in plane] + [hop("z", d) for d in range(1, nz)] + [hop("core", 1)]
    for peer in peers:
        pl.semaphore_signal(barrier, inc=1, device_id=peer, device_id_type=pl.DeviceIdType.MESH)

    y_order = far_first(ny) + [0]
    loads = {}
    for n, d in enumerate(y_order):
        u = lax.rem(y + d, ny)
        loads[d] = [
            pltpu.make_async_copy(mom_hbm.at[u], mom.at[d], in_s.at[0, d]),
            pltpu.make_async_copy(grad_hbm.at[u], grad.at[d], in_s.at[1, d]),
        ]
        for go in loads[d]:
            go.start()
        if n == 0:
            load_basis = pltpu.make_async_copy(basis_hbm, basis, in_s.at[2, 0])
            load_basis.start()
    load_basis_wait = [load_basis]

    pending = []

    def partial_rows(d):
        for go in loads[d] + load_basis_wait:
            go.wait()
        load_basis_wait.clear()
        rows = (mom[d].astype(F32) + grad[d].astype(F32)).astype(BF16)
        buf[lax.rem(y + d, ny)] = rows
        return dot(rows, basis[...])

    def start_scatter(axis, n, send, rx, sems):
        me, size = {"x": (x, nx), "y": (y, ny), "z": (z, nz)}[axis]
        copies = []
        for d in far_first(size):
            src = send.at[lax.rem(me + d, size)]
            go = copy(src, rx.at[d - 1], sems[0].at[n, d - 1], sems[1].at[n, d - 1], hop(axis, d))
            go.start()
            copies.append(go)
        return copies

    def start_exchange(axis, n, send, rx, sems):
        size = {"x": nx, "y": ny, "z": nz}[axis]
        copies = []
        for d in far_first(size):
            go = copy(send, rx.at[d - 1], sems[0].at[n, d - 1], sems[1].at[n, d - 1], hop(axis, d))
            go.start()
            copies.append(go)
        return copies

    def arrived(copies):
        for go in copies:
            go.wait_recv()
        pending.extend(copies)

    def start_gather(axis, n, view, sems):
        me, size = {"x": (x, nx), "y": (y, ny), "z": (z, nz)}[axis]
        copies = []
        for d in far_first(size):
            go = copy(view(me), view(me), sems[0].at[n, d - 1], sems[1].at[n, d - 1], hop(axis, d))
            go.start()
            copies.append(go)
        return copies

    def gathered(axis, n, view, copies, sems):
        me, size = {"x": (x, nx), "y": (y, ny), "z": (z, nz)}[axis]
        for d in far_first(size):
            src = lax.rem(me - d + size, size)
            copy(view(src), view(src), sems[0].at[n, d - 1], sems[1].at[n, d - 1], hop(axis, d)).wait_recv()
        pending.extend(copies)

    xs, ys, zs = (x_s, x_r), (y_s, y_r), (z_s, z_r)

    for d in y_order[:-1]:
        p_part[d - 1] = partial_rows(d).astype(BF16)
    pl.semaphore_wait(barrier, len(peers))
    rank = p_sum.shape[2]
    sides = [pl.ds(0, rank // 2), pl.ds(rank // 2, rank // 2)]
    p_go = []
    for n, side in enumerate(sides):
        p_go.append([])
        for d in y_order[:-1]:
            go = copy(p_part.at[d - 1, :, side], p_rx.at[d - 1, :, side],
                      y_s.at[n, d - 1], y_r.at[n, d - 1], hop("y", d))
            go.start()
            p_go[n].append(go)
    own = partial_rows(0)
    p_gather = []
    for n, side in enumerate(sides):
        arrived(p_go[n])
        total = own[:, n * rank // 2:(n + 1) * rank // 2]
        for d in y_order[:-1]:
            total = total + p_rx[d - 1, :, side].astype(F32)
        p_sum[y, :, side] = total.astype(BF16)
        p_gather.append(start_gather("y", 2 + n, lambda i: p_sum.at[i, :, side], ys))
    for n, side in enumerate(sides):
        gathered("y", 2 + n, lambda i: p_sum.at[i, :, side], p_gather[n], ys)

    rows = buf.shape[0] * buf.shape[1]
    half = rank // 2
    p_all = p_sum[...].reshape(rows, rank)
    p_t[...] = p_all.T.reshape(2, half, rows)
    gcols = rank // ny

    p_cols = [p_all[:, gcols * i: gcols * (i + 1)] for i in range(ny)]
    p_mine = p_cols[0]
    for i in range(1, ny):
        p_mine = jnp.where(y == i, p_cols[i], p_mine)
    g_send[...] = dot(p_t[other], p_mine).reshape(g_send.shape)
    g_go = copy(g_send, g_core, core_s.at[0], core_r.at[0], hop("core", 1))
    g_go.start()

    pieces, _, _, tr, cb = t_send.shape
    t_shape = (pieces, nx, tr, cb)
    for k in range(nz):
        cols = buf[:, :, cb * k: cb * (k + 1)].reshape(rows, cb)
        t_send[:, :, k] = dot(p_t[other], cols).astype(BF16).reshape(t_shape)
    t_core_go = []
    for p in range(pieces):
        go = copy(t_send.at[p], t_core.at[p], core_s.at[2 + p], core_r.at[2 + p], hop("core", 1))
        go.start()
        t_core_go.append(go)
    g_own[...] = dot(p_t[c], p_mine).reshape(g_own.shape)
    arrived([g_go])
    g_xs[...] = g_own[...] + g_core[...]
    g_x = start_scatter("x", 0, g_xs, g_xrx, xs)

    for k in range(nz):
        cols = buf[:, :, cb * k: cb * (k + 1)].reshape(rows, cb)
        t_own[:, :, k] = dot(p_t[c], cols).reshape(t_shape)

    t_go = {}

    def sum_core(p):
        arrived([t_core_go[p]])
        total = t_own[p] + t_core[p].astype(F32)
        t_own[p] = total
        t_xs[p] = total.astype(BF16)
        t_go["x", p] = start_scatter("x", 1 + p, t_xs.at[p], t_xrx.at[p], xs)

    def sum_x(p):
        arrived(t_go["x", p])
        total = t_own[p, x]
        for d in range(nx - 1):
            total = total + t_xrx[p, d].astype(F32)
        t_zf[p] = total
        t_zs[p] = total.astype(BF16)
        t_go["z", p] = start_scatter("z", 2 + p, t_zs.at[p], t_zrx.at[p], zs)

    def sum_z(p):
        arrived(t_go["z", p])
        total = t_zf[p, z]
        for d in range(nz - 1):
            total = total + t_zrx[p, d].astype(F32)
        t_all[c, p, x, z] = total.astype(BF16)
        t_go["gz", p] = start_gather("z", 2 + pieces + p, lambda i: t_all.at[c, p, x, i], zs)

    def gather_x(p):
        gathered("z", 2 + pieces + p, lambda i: t_all.at[c, p, x, i], t_go["gz", p], zs)
        t_go["gx", p] = start_gather("x", 1 + pieces + p, lambda i: t_all.at[c, p, i], xs)

    def gather_core(p):
        gathered("x", 1 + pieces + p, lambda i: t_all.at[c, p, i], t_go["gx", p], xs)
        t_go["gc", p] = copy(t_all.at[c, p], t_all.at[c, p], core_s.at[2 + pieces + p],
                             core_r.at[2 + pieces + p], hop("core", 1))
        t_go["gc", p].start()

    def got_core(p):
        part = t_all.at[other, p]
        copy(part, part, core_s.at[2 + pieces + p], core_r.at[2 + pieces + p], hop("core", 1)).wait_recv()
        pending.append(t_go["gc", p])

    for p in range(pieces):
        sum_core(p)
    arrived(g_x)
    g_zs[...] = sum((g_xrx[d] for d in range(nx - 1)), g_xs[x])
    parts = [pl.ds(0, nz // 2), pl.ds(nz // 2, nz // 2)]
    g_z = [start_exchange("z", n, g_zs.at[part], g_zrx.at[:, part], zs) for n, part in enumerate(parts)]

    nb = rank // 128
    row = lax.broadcasted_iota(jnp.int32, (128, 128), 0)
    col = lax.broadcasted_iota(jnp.int32, (128, 128), 1)
    eye = jnp.where(row == col, 1.0, 0.0)
    for i in range(nb):
        for j in range(nb):
            m[128 * i:128 * (i + 1), rank + 128 * j:rank + 128 * (j + 1)] = eye if i == j else jnp.zeros_like(eye)

    g_xy = []
    for h, part in enumerate(parts):
        sum_x(h)
        arrived(g_z[h])
        g_all[c, x, y, part] = sum((g_zrx[d, part] for d in range(nz - 1)), g_zs[part])
        for n, d in enumerate(plane):
            mine = g_all.at[c, x, y, part]
            go = copy(mine, mine, xy_s.at[h, n], xy_r.at[h, n], hop("xy", d))
            go.start()
            g_xy.append(go)
    sum_x(2)
    sum_z(0)
    sum_x(3)
    sum_z(1)
    gather_x(0)
    sum_z(2)
    g_core_go = []
    for h, part in enumerate(parts):
        for n, d in enumerate(plane):
            theirs = g_all.at[c, lax.rem(x - d[0] + nx, nx), lax.rem(y - d[1] + ny, ny), part]
            copy(theirs, theirs, xy_s.at[h, n], xy_r.at[h, n], hop("xy", d)).wait_recv()
        half_sem = [1, 2 + 2 * pieces][h]
        mine = g_all.at[c, :, :, part]
        go = copy(mine, mine, core_s.at[half_sem], core_r.at[half_sem], hop("core", 1))
        go.start()
        g_core_go.append(go)
    pending += g_xy
    sum_z(3)
    gather_x(1)
    for h, part in enumerate(parts):
        half_sem = [1, 2 + 2 * pieces][h]
        theirs = g_all.at[other, :, :, part]
        copy(theirs, theirs, core_s.at[half_sem], core_r.at[half_sem], hop("core", 1)).wait_recv()
    pending += g_core_go

    gr = g_all.shape[3] * g_all.shape[4]
    for i in range(2):
        for j in range(nx):
            for k in range(ny):
                lo = (i * nx + j) * gr
                m[lo:lo + gr, gcols * k:gcols * (k + 1)] = g_all[i, j, k].reshape(gr, gcols)
    plan = {3: (gather_x, 2), 8: (gather_core, 0), 14: (gather_x, 3), 20: (gather_core, 1),
            30: (gather_core, 2), 42: (gather_core, 3)}
    plan = {at_step * nb // 4: stage for at_step, stage in plan.items()}
    assert len(plan) == 6 and pieces == 4
    for k in range(nb):
        lo, hi = 128 * k, 128 * (k + 1)
        w[:, 0:128] = m[lo:hi, lo:hi]
        w[:, 128:256] = eye
        factor128(w, {n - 16 * k: f for n, f in plan.items()})
        inv = w[:, 128:256]
        m[lo:hi, hi:rank + hi] = dot(inv, m[lo:hi, hi:rank + hi], precision=HIGHEST)
        if k + 1 < nb:
            m[hi:, hi:rank + hi] = m[hi:, hi:rank + hi] - dot(
                m[lo:hi, hi:rank], m[lo:hi, hi:rank + hi], ((0,), (0,)), HIGHEST)
    high, low = split(m[:, rank:])
    both = jnp.concatenate([high, low], axis=0)
    for p in range(pieces):
        got_core(p)

    total = jnp.zeros((rank, 128), F32)
    for k in range(nz):
        r = dot(both, t_all[:, :, :, k].reshape(rank, cb))
        r = r[:rank] + r[rank:]
        r_f32[:, cb * k:cb * (k + 1)] = r
        for i in range(cb // 128):
            part = r[:, 128 * i:128 * (i + 1)]
            total = total + part * part
    sq_own[...] = dot(jnp.ones((8, 128), F32), total, ((1,), (1,)), HIGHEST)
    sq_go = start_exchange("y", 4, sq_own, sq_rx, ys)
    orth = (dot(p_all, high, ((1,), (1,))) + dot(p_all, low, ((1,), (1,)))).astype(BF16)
    orth_ref[...] = orth
    for k in range(nz):
        place = pl.ds(cb * k, cb)
        low_rank = dot(orth, r_f32[:, place].astype(BF16))
        mom_ref[:, place] = (buf[:, :, place].reshape(rows, cb).astype(F32) - 0.05 * low_rank).astype(BF16)
    arrived(sq_go)
    total = sum((sq_rx[d] for d in range(ny - 1)), sq_own[...])
    scale = lax.rsqrt(total / cols_total + 1e-06)
    scale = dot(scale, jnp.full((8, 128), 0.125, F32), ((0,), (0,)), HIGHEST)
    for k in range(nz * cb // 128):
        part = pl.ds(128 * k, 128)
        nb_ref[:, part] = (r_f32[:, part] * scale).astype(BF16)
    for go in pending:
        go.wait_send()


def update_call(shape, cols_total, mom, grad, basis):
    nx, nz, ny = shape
    rows, cols = mom.shape
    rank = basis.shape[1]
    part, cb, gb = rows // ny, cols // nz, rank // (2 * nx * nz)
    gc, np = rank // ny, PIECES
    tr = rank // (2 * np * nx)
    args = (mom.reshape(ny, part, cols), grad.reshape(ny, part, cols), basis)
    vmem, sem = pltpu.VMEM, pltpu.SemaphoreType.DMA
    space = pl.BlockSpec(memory_space=pltpu.VMEM)
    hbm = pl.BlockSpec(memory_space=pltpu.MemorySpace.HBM)
    return pl.pallas_call(
        functools.partial(update_kernel, shape, cols_total),
        out_shape=(
            vmem((rows, rank), BF16),
            vmem((rows, cols), BF16),
            vmem((rank, cols), BF16),
        ),
        in_specs=[hbm] * 3,
        out_specs=(space,) * 3,
        scratch_shapes=[
            vmem((ny, part, cols), BF16),
            vmem((ny, part, cols), BF16),
            vmem((ny, part, cols), BF16),
            vmem((cols, rank), BF16),
            vmem((ny - 1, part, rank), BF16),
            vmem((ny - 1, part, rank), BF16),
            vmem((ny, part, rank), BF16),
            vmem((2, rank // 2, rows), BF16),
            vmem((nx, nz, gb, gc), F32),
            vmem((nx, nz, gb, gc), F32),
            vmem((nx, nz, gb, gc), F32),
            vmem((nx, nz, gb, gc), F32),
            vmem((nx - 1, nz, gb, gc), F32),
            vmem((nz, gb, gc), F32),
            vmem((nz - 1, nz, gb, gc), F32),
            vmem((2, nx, ny, nz, gb, gc), F32),
            vmem((np, nx, nz, tr, cb), BF16),
            vmem((np, nx, nz, tr, cb), F32),
            vmem((np, nx, nz, tr, cb), BF16),
            vmem((np, nx, nz, tr, cb), BF16),
            vmem((np, nx - 1, nz, tr, cb), BF16),
            vmem((np, nz, tr, cb), F32),
            vmem((np, nz, tr, cb), BF16),
            vmem((np, nz - 1, tr, cb), BF16),
            vmem((2, np, nx, nz, tr, cb), BF16),
            vmem((rank, cols), F32),
            vmem((rank, 2 * rank), F32),
            vmem((128, 256), F32),
            vmem((8, rank), F32),
            vmem((ny - 1, 8, rank), F32),
            sem((3, ny)),
            sem((3 + 2 * np,)), sem((3 + 2 * np,)),
            sem((1 + 2 * np, nx - 1)), sem((1 + 2 * np, nx - 1)),
            sem((5, ny - 1)), sem((5, ny - 1)),
            sem((2 + 2 * np, nz - 1)), sem((2 + 2 * np, nz - 1)),
            sem((2, nx * ny - 1)), sem((2, nx * ny - 1)),
        ],
        compiler_params=pltpu.CompilerParams(
            collective_id=0, has_side_effects=True, vmem_limit_bytes=VMEM_LIMIT),
        name="update",
    )(*(pltpu.with_memory_space_constraint(v, pltpu.MemorySpace.HBM) for v in args))


def factor8(cols):
    e = [[jnp.broadcast_to(cols[k][q:q + 1, :], (8, 128)) for k in range(q + 1)] for q in range(8)]
    low = [[None] * 8 for _ in range(8)]
    inv = [[None] * 8 for _ in range(8)]
    for p in range(8):
        inv[p][p] = lax.rsqrt(e[p][p])
        for q in range(p + 1, 8):
            low[q][p] = e[q][p] * inv[p][p]
        for q in range(p + 1, 8):
            for k in range(p + 1, q + 1):
                e[q][k] = e[q][k] - low[q][p] * low[k][p]
    for q in range(8):
        for k in range(q):
            acc = low[q][k] * inv[k][k]
            for m in range(k + 1, q):
                acc = acc + low[q][m] * inv[m][k]
            inv[q][k] = -acc * inv[q][q]
    return inv


def lanes(x, k):
    return jnp.broadcast_to(x[:, k:k + 1], (8, 128))


def rows8(x, k):
    return jnp.broadcast_to(x[k:k + 1, :], (8, 128))


def split3(x):
    high = x.astype(BF16).astype(F32)
    x = x - high
    mid = x.astype(BF16).astype(F32)
    return high, mid, x - mid


def rank8(a, v):
    ha, ma, la = split3(a)
    hv, mv, lv = split3(v)
    left = jnp.concatenate([ha, ma, la, ha, ma, ha], axis=0).astype(BF16)
    right_a = jnp.concatenate([ha, ha, ha, ma, ma, la], axis=0)
    right_v = jnp.concatenate([hv, hv, hv, mv, mv, lv], axis=0)
    return dot(left, jnp.concatenate([right_a, right_v], axis=1).astype(BF16), ((0,), (0,)))


def factor128(r, between):
    sub = lax.broadcasted_iota(jnp.int32, (8, 128), 0)
    a, v = r[0:8, 0:128], r[0:8, 128:256]
    cols = [lanes(a, k) for k in range(8)]
    for s in range(16):
        if s in between:
            between[s][0](between[s][1])
        lo = 8 * s
        if s < 15:
            an, vn = r[lo + 8:lo + 16, 0:128], r[lo + 8:lo + 16, 128:256]
            below = [lanes(an, lo + k) for k in range(8)]
            ahead = [lanes(an, lo + 8 + k) for k in range(8)]
        inv = factor8(cols)
        new_a = new_v = None
        for k in range(8):
            m = jnp.where(sub == k, inv[k][k], 0.0)
            for q in range(k + 1, 8):
                m = jnp.where(sub == q, inv[q][k], m)
            ta, tv = m * rows8(a, k), m * rows8(v, k)
            new_a = ta if new_a is None else new_a + ta
            new_v = tv if new_v is None else new_v + tv
        r[lo:lo + 8, 128:256] = new_v
        if s < 15:
            low = []
            for k in range(8):
                acc = below[0] * inv[k][0]
                for j in range(1, k + 1):
                    acc = acc + below[j] * inv[k][j]
                low.append(acc)
            cols = []
            for k in range(8):
                an = an - low[k] * rows8(new_a, k)
                vn = vn - low[k] * rows8(new_v, k)
                acc = ahead[k]
                for j in range(8):
                    acc = acc - low[j] * rows8(low[j], k)
                cols.append(acc)
            a, v = an, vn
        if s < 14:
            r[lo + 16:128, :] = r[lo + 16:128, :] - rank8(new_a, new_v)[lo + 16:128, :]


def split(x):
    high = x.astype(BF16)
    return high, (x - high.astype(F32)).astype(BF16)


def outputs_kernel(orth, new_mom, nb_t, mom_hbm, basis_hbm, dir_hbm, basis_out, dir_out, sems):
    blocks, rows, wide = dir_out.shape
    factor = orth[...]
    copies = [pltpu.make_async_copy(new_mom, mom_hbm, sems.at[2, 0])]
    copies[0].start()
    for i in range(blocks):
        place = pl.ds(i * wide, wide)
        new_basis = nb_t[:, place]
        dir_out[i] = (math.sqrt(ROWS / RANK) * dot(factor, new_basis)).astype(BF16)
        basis_out[place, :] = new_basis.T
        for n, (src, dst) in enumerate((
            (dir_out.at[i], dir_hbm.at[:, place]),
            (basis_out.at[place, :], basis_hbm.at[place, :]),
        )):
            go = pltpu.make_async_copy(src, dst, sems.at[n, i])
            go.start()
            copies.append(go)
    for go in copies:
        go.wait()


def outputs_call(orth, new_mom, nb_t):
    rows, cols = new_mom.shape
    rank = orth.shape[1]
    wide = 256
    blocks = cols // wide
    space = pl.BlockSpec(memory_space=pltpu.VMEM)
    hbm = pl.BlockSpec(memory_space=pl.ANY)
    args = [pltpu.with_memory_space_constraint(v, pltpu.VMEM) for v in (orth, new_mom, nb_t)]
    return pl.pallas_call(
        outputs_kernel,
        out_shape=(
            jax.ShapeDtypeStruct((rows, cols), BF16),
            jax.ShapeDtypeStruct((cols, rank), BF16),
            jax.ShapeDtypeStruct((rows, cols), BF16),
        ),
        in_specs=[space] * 3,
        out_specs=(hbm,) * 3,
        scratch_shapes=[
            pltpu.VMEM((cols, rank), BF16),
            pltpu.VMEM((blocks, rows, wide), BF16),
            pltpu.SemaphoreType.DMA((3, blocks)),
        ],
        compiler_params=pltpu.CompilerParams(vmem_limit_bytes=VMEM_LIMIT),
        name="outputs",
    )(*args)


def per_device(momentum, gradient, old_basis):
    orth, new_momentum, basis_t = update_call(SHAPE, COLS, momentum, gradient, old_basis)
    return outputs_call(orth, new_momentum, basis_t)


def solution(mesh):
    in_specs = (P("zero", "tensor"), P("zero", "tensor"), P("tensor", None))
    out_specs = (P("zero", "tensor"), P("tensor", None), P("zero", "tensor"))
    return jax.shard_map(
        per_device, mesh=mesh, in_specs=in_specs, out_specs=out_specs, check_vma=False
    )
```

```python
import functools
import math

import jax
import jax.numpy as jnp
from jax import lax
from jax.experimental import pallas as pl
from jax.experimental.pallas import tpu as pltpu
from jax.sharding import PartitionSpec as P

ROWS = 28672
COLS = 8192
RANK = 512
F32 = jnp.float32
BF16 = jnp.bfloat16
HIGHEST = lax.Precision.HIGHEST
SHAPE = (4, 8, 4)
VMEM_LIMIT = 40 * 1024 * 1024
PIECES = 4


def dot(a, b, contract=((1,), (0,)), precision=None):
    return lax.dot_general(
        a, b, (contract, ((), ())), precision=precision, preferred_element_type=F32
    )


def update_kernel(shape, cols_total, mom_hbm, grad_hbm, basis_hbm, orth_ref, mom_ref, nb_ref,
                  buf, mom, grad, basis, p_part, p_rx, p_sum, p_t,
                  g_send, g_own, g_core, g_xs, g_xrx, g_zs, g_zrx, g_all,
                  t_send, t_own, t_core, t_xs, t_xrx, t_zf, t_zs, t_zrx, t_all,
                  r_f32, m, w, sq_own, sq_rx, in_s, core_s, core_r, x_s, x_r, y_s, y_r, z_s, z_r, xy_s, xy_r):
    nx, nz, ny = shape
    zero, y = lax.axis_index("zero"), lax.axis_index("tensor")
    c = lax.rem(zero, 2)
    z = lax.rem(lax.div(zero, 2), nz)
    x = lax.div(zero, 2 * nz)
    other = 1 - c

    def at(xx, zz, cc):
        return (xx * nz + zz) * 2 + cc

    def hop(axis, d):
        if axis == "x":
            return (at(lax.rem(x + d, nx), z, c), y)
        if axis == "z":
            return (at(x, lax.rem(z + d, nz), c), y)
        if axis == "y":
            return (zero, lax.rem(y + d, ny))
        if axis == "xy":
            return (at(lax.rem(x + d[0], nx), z, c), lax.rem(y + d[1], ny))
        return (at(x, z, other), y)

    def copy(src, dst, send, recv, device):
        return pltpu.make_async_remote_copy(
            src_ref=src, dst_ref=dst, send_sem=send, recv_sem=recv,
            device_id=device, device_id_type=pl.DeviceIdType.MESH)

    def far_first(size):
        return sorted(range(1, size), key=lambda d: -min(d, size - d))

    plane = [(i, j) for i in range(nx) for j in range(ny) if i or j]
    plane.sort(key=lambda d: -(min(d[0], nx - d[0]) + min(d[1], ny - d[1])))
    barrier = pltpu.get_barrier_semaphore()
    peers = [hop("xy", d) for d in plane] + [hop("z", d) for d in range(1, nz)] + [hop("core", 1)]
    for peer in peers:
        pl.semaphore_signal(barrier, inc=1, device_id=peer, device_id_type=pl.DeviceIdType.MESH)

    y_order = far_first(ny) + [0]
    loads = {}
    for n, d in enumerate(y_order):
        u = lax.rem(y + d, ny)
        loads[d] = [
            pltpu.make_async_copy(mom_hbm.at[u], mom.at[d], in_s.at[0, d]),
            pltpu.make_async_copy(grad_hbm.at[u], grad.at[d], in_s.at[1, d]),
        ]
        for go in loads[d]:
            go.start()
        if n == 0:
            load_basis = pltpu.make_async_copy(basis_hbm, basis, in_s.at[2, 0])
            load_basis.start()
    load_basis_wait = [load_basis]

    pending = []

    def partial_rows(d):
        for go in loads[d] + load_basis_wait:
            go.wait()
        load_basis_wait.clear()
        rows = (mom[d].astype(F32) + grad[d].astype(F32)).astype(BF16)
        buf[lax.rem(y + d, ny)] = rows
        return dot(rows, basis[...])

    def start_scatter(axis, n, send, rx, sems):
        me, size = {"x": (x, nx), "y": (y, ny), "z": (z, nz)}[axis]
        copies = []
        for d in far_first(size):
            src = send.at[lax.rem(me + d, size)]
            go = copy(src, rx.at[d - 1], sems[0].at[n, d - 1], sems[1].at[n, d - 1], hop(axis, d))
            go.start()
            copies.append(go)
        return copies

    def start_exchange(axis, n, send, rx, sems):
        size = {"x": nx, "y": ny, "z": nz}[axis]
        copies = []
        for d in far_first(size):
            go = copy(send, rx.at[d - 1], sems[0].at[n, d - 1], sems[1].at[n, d - 1], hop(axis, d))
            go.start()
            copies.append(go)
        return copies

    def arrived(copies):
        for go in copies:
            go.wait_recv()
        pending.extend(copies)

    def start_gather(axis, n, view, sems):
        me, size = {"x": (x, nx), "y": (y, ny), "z": (z, nz)}[axis]
        copies = []
        for d in far_first(size):
            go = copy(view(me), view(me), sems[0].at[n, d - 1], sems[1].at[n, d - 1], hop(axis, d))
            go.start()
            copies.append(go)
        return copies

    def gathered(axis, n, view, copies, sems):
        me, size = {"x": (x, nx), "y": (y, ny), "z": (z, nz)}[axis]
        for d in far_first(size):
            src = lax.rem(me - d + size, size)
            copy(view(src), view(src), sems[0].at[n, d - 1], sems[1].at[n, d - 1], hop(axis, d)).wait_recv()
        pending.extend(copies)

    xs, ys, zs = (x_s, x_r), (y_s, y_r), (z_s, z_r)

    for d in y_order[:-1]:
        p_part[d - 1] = partial_rows(d).astype(BF16)
    pl.semaphore_wait(barrier, len(peers))
    rank = p_sum.shape[2]
    quarter = rank // 4
    sides = [pl.ds(n * quarter, quarter) for n in range(4)]
    p_go = []
    for n, side in enumerate(sides):
        p_go.append([])
        for d in y_order[:-1]:
            go = copy(p_part.at[d - 1, :, side], p_rx.at[d - 1, :, side],
                      y_s.at[n, d - 1], y_r.at[n, d - 1], hop("y", d))
            go.start()
            p_go[n].append(go)
    own = partial_rows(0)
    p_gather = []
    for n, side in enumerate(sides):
        arrived(p_go[n])
        total = own[:, n * quarter:(n + 1) * quarter]
        for d in y_order[:-1]:
            total = total + p_rx[d - 1, :, side].astype(F32)
        p_sum[y, :, side] = total.astype(BF16)
        p_gather.append(start_gather("y", 4 + n, lambda i: p_sum.at[i, :, side], ys))
    for n, side in enumerate(sides):
        gathered("y", 4 + n, lambda i: p_sum.at[i, :, side], p_gather[n], ys)

    rows = buf.shape[0] * buf.shape[1]
    half = rank // 2
    p_all = p_sum[...].reshape(rows, rank)
    p_t[...] = p_all.T.reshape(2, half, rows)
    gcols = rank // ny

    p_cols = [p_all[:, gcols * i: gcols * (i + 1)] for i in range(ny)]
    p_mine = p_cols[0]
    for i in range(1, ny):
        p_mine = jnp.where(y == i, p_cols[i], p_mine)
    g_send[...] = dot(p_t[other], p_mine).reshape(g_send.shape)
    g_go = copy(g_send, g_core, core_s.at[0], core_r.at[0], hop("core", 1))
    g_go.start()

    pieces, _, _, tr, cb = t_send.shape
    t_shape = (pieces, nx, tr, cb)
    for k in range(nz):
        cols = buf[:, :, cb * k: cb * (k + 1)].reshape(rows, cb)
        t_send[:, :, k] = dot(p_t[other], cols).astype(BF16).reshape(t_shape)
    t_core_go = []
    for p in range(pieces):
        go = copy(t_send.at[p], t_core.at[p], core_s.at[2 + p], core_r.at[2 + p], hop("core", 1))
        go.start()
        t_core_go.append(go)
    g_own[...] = dot(p_t[c], p_mine).reshape(g_own.shape)
    arrived([g_go])
    g_xs[...] = g_own[...] + g_core[...]
    g_x = start_scatter("x", 0, g_xs, g_xrx, xs)

    for k in range(nz):
        cols = buf[:, :, cb * k: cb * (k + 1)].reshape(rows, cb)
        t_own[:, :, k] = dot(p_t[c], cols).reshape(t_shape)

    t_go = {}

    def sum_core(p):
        arrived([t_core_go[p]])
        total = t_own[p] + t_core[p].astype(F32)
        t_own[p] = total
        t_xs[p] = total.astype(BF16)
        t_go["x", p] = start_scatter("x", 1 + p, t_xs.at[p], t_xrx.at[p], xs)

    def sum_x(p):
        arrived(t_go["x", p])
        total = t_own[p, x]
        for d in range(nx - 1):
            total = total + t_xrx[p, d].astype(F32)
        t_zf[p] = total
        t_zs[p] = total.astype(BF16)
        t_go["z", p] = start_scatter("z", 2 + p, t_zs.at[p], t_zrx.at[p], zs)

    def sum_z(p):
        arrived(t_go["z", p])
        total = t_zf[p, z]
        for d in range(nz - 1):
            total = total + t_zrx[p, d].astype(F32)
        t_all[c, p, x, z] = total.astype(BF16)
        t_go["gz", p] = start_gather("z", 2 + pieces + p, lambda i: t_all.at[c, p, x, i], zs)

    def gather_x(p):
        gathered("z", 2 + pieces + p, lambda i: t_all.at[c, p, x, i], t_go["gz", p], zs)
        t_go["gx", p] = start_gather("x", 1 + pieces + p, lambda i: t_all.at[c, p, i], xs)

    def gather_core(p):
        gathered("x", 1 + pieces + p, lambda i: t_all.at[c, p, i], t_go["gx", p], xs)
        t_go["gc", p] = copy(t_all.at[c, p], t_all.at[c, p], core_s.at[2 + pieces + p],
                             core_r.at[2 + pieces + p], hop("core", 1))
        t_go["gc", p].start()

    def got_core(p):
        part = t_all.at[other, p]
        copy(part, part, core_s.at[2 + pieces + p], core_r.at[2 + pieces + p], hop("core", 1)).wait_recv()
        pending.append(t_go["gc", p])

    for p in range(pieces):
        sum_core(p)
    arrived(g_x)
    g_zs[...] = sum((g_xrx[d] for d in range(nx - 1)), g_xs[x])
    parts = [pl.ds(0, nz // 2), pl.ds(nz // 2, nz // 2)]
    g_z = [start_exchange("z", n, g_zs.at[part], g_zrx.at[:, part], zs) for n, part in enumerate(parts)]

    nb = rank // 128
    row = lax.broadcasted_iota(jnp.int32, (128, 128), 0)
    col = lax.broadcasted_iota(jnp.int32, (128, 128), 1)
    eye = jnp.where(row == col, 1.0, 0.0)
    for i in range(nb):
        for j in range(nb):
            m[128 * i:128 * (i + 1), rank + 128 * j:rank + 128 * (j + 1)] = eye if i == j else jnp.zeros_like(eye)

    g_xy = []
    for h, part in enumerate(parts):
        sum_x(h)
        arrived(g_z[h])
        g_all[c, x, y, part] = sum((g_zrx[d, part] for d in range(nz - 1)), g_zs[part])
        for n, d in enumerate(plane):
            mine = g_all.at[c, x, y, part]
            go = copy(mine, mine, xy_s.at[h, n], xy_r.at[h, n], hop("xy", d))
            go.start()
            g_xy.append(go)
    sum_x(2)
    sum_z(0)
    sum_x(3)
    sum_z(1)
    gather_x(0)
    sum_z(2)
    g_core_go = []
    for h, part in enumerate(parts):
        for n, d in enumerate(plane):
            theirs = g_all.at[c, lax.rem(x - d[0] + nx, nx), lax.rem(y - d[1] + ny, ny), part]
            copy(theirs, theirs, xy_s.at[h, n], xy_r.at[h, n], hop("xy", d)).wait_recv()
        half_sem = [1, 2 + 2 * pieces][h]
        mine = g_all.at[c, :, :, part]
        go = copy(mine, mine, core_s.at[half_sem], core_r.at[half_sem], hop("core", 1))
        go.start()
        g_core_go.append(go)
    pending += g_xy
    sum_z(3)
    gather_x(1)
    for h, part in enumerate(parts):
        half_sem = [1, 2 + 2 * pieces][h]
        theirs = g_all.at[other, :, :, part]
        copy(theirs, theirs, core_s.at[half_sem], core_r.at[half_sem], hop("core", 1)).wait_recv()
    pending += g_core_go

    gr = g_all.shape[3] * g_all.shape[4]
    for i in range(2):
        for j in range(nx):
            for k in range(ny):
                lo = (i * nx + j) * gr
                m[lo:lo + gr, gcols * k:gcols * (k + 1)] = g_all[i, j, k].reshape(gr, gcols)
    plan = {12: (gather_x, 2), 20: (gather_x, 3), 30: (gather_core, 0), 40: (gather_core, 1),
            52: (gather_core, 2), 62: (gather_core, 3)}
    plan = {at_step * nb // 4: stage for at_step, stage in plan.items()}
    assert len(plan) == 6 and pieces == 4
    for k in range(nb):
        lo, hi = 128 * k, 128 * (k + 1)
        w[:, 0:128] = m[lo:hi, lo:hi]
        w[:, 128:256] = eye
        factor128(w, {n - 16 * k: f for n, f in plan.items()})
        inv = w[:, 128:256]
        m[lo:hi, hi:rank + hi] = dot(inv, m[lo:hi, hi:rank + hi], precision=HIGHEST)
        if k + 1 < nb:
            m[hi:, hi:rank + hi] = m[hi:, hi:rank + hi] - dot(
                m[lo:hi, hi:rank], m[lo:hi, hi:rank + hi], ((0,), (0,)), HIGHEST)
    high, low = split(m[:, rank:])
    both = jnp.concatenate([high, low], axis=0)
    for p in range(pieces):
        got_core(p)

    total = jnp.zeros((rank, 128), F32)
    for k in range(nz):
        r = dot(both, t_all[:, :, :, k].reshape(rank, cb))
        r = r[:rank] + r[rank:]
        r_f32[:, cb * k:cb * (k + 1)] = r
        for i in range(cb // 128):
            part = r[:, 128 * i:128 * (i + 1)]
            total = total + part * part
    sq_own[...] = dot(jnp.ones((8, 128), F32), total, ((1,), (1,)), HIGHEST)
    sq_go = start_exchange("y", 8, sq_own, sq_rx, ys)
    orth = (dot(p_all, high, ((1,), (1,))) + dot(p_all, low, ((1,), (1,)))).astype(BF16)
    orth_ref[...] = orth
    for k in range(nz):
        place = pl.ds(cb * k, cb)
        low_rank = dot(orth, r_f32[:, place].astype(BF16))
        mom_ref[:, place] = (buf[:, :, place].reshape(rows, cb).astype(F32) - 0.05 * low_rank).astype(BF16)
    arrived(sq_go)
    total = sum((sq_rx[d] for d in range(ny - 1)), sq_own[...])
    scale = lax.rsqrt(total / cols_total + 1e-06)
    scale = dot(scale, jnp.full((8, 128), 0.125, F32), ((0,), (0,)), HIGHEST)
    for k in range(nz * cb // 128):
        part = pl.ds(128 * k, 128)
        nb_ref[:, part] = (r_f32[:, part] * scale).astype(BF16)
    for go in pending:
        go.wait_send()


def update_call(shape, cols_total, mom, grad, basis):
    nx, nz, ny = shape
    rows, cols = mom.shape
    rank = basis.shape[1]
    part, cb, gb = rows // ny, cols // nz, rank // (2 * nx * nz)
    gc, np = rank // ny, PIECES
    tr = rank // (2 * np * nx)
    args = (mom.reshape(ny, part, cols), grad.reshape(ny, part, cols), basis)
    vmem, sem = pltpu.VMEM, pltpu.SemaphoreType.DMA
    space = pl.BlockSpec(memory_space=pltpu.VMEM)
    hbm = pl.BlockSpec(memory_space=pltpu.MemorySpace.HBM)
    return pl.pallas_call(
        functools.partial(update_kernel, shape, cols_total),
        out_shape=(
            vmem((rows, rank), BF16),
            vmem((rows, cols), BF16),
            vmem((rank, cols), BF16),
        ),
        in_specs=[hbm] * 3,
        out_specs=(space,) * 3,
        scratch_shapes=[
            vmem((ny, part, cols), BF16),
            vmem((ny, part, cols), BF16),
            vmem((ny, part, cols), BF16),
            vmem((cols, rank), BF16),
            vmem((ny - 1, part, rank), BF16),
            vmem((ny - 1, part, rank), BF16),
            vmem((ny, part, rank), BF16),
            vmem((2, rank // 2, rows), BF16),
            vmem((nx, nz, gb, gc), F32),
            vmem((nx, nz, gb, gc), F32),
            vmem((nx, nz, gb, gc), F32),
            vmem((nx, nz, gb, gc), F32),
            vmem((nx - 1, nz, gb, gc), F32),
            vmem((nz, gb, gc), F32),
            vmem((nz - 1, nz, gb, gc), F32),
            vmem((2, nx, ny, nz, gb, gc), F32),
            vmem((np, nx, nz, tr, cb), BF16),
            vmem((np, nx, nz, tr, cb), F32),
            vmem((np, nx, nz, tr, cb), BF16),
            vmem((np, nx, nz, tr, cb), BF16),
            vmem((np, nx - 1, nz, tr, cb), BF16),
            vmem((np, nz, tr, cb), F32),
            vmem((np, nz, tr, cb), BF16),
            vmem((np, nz - 1, tr, cb), BF16),
            vmem((2, np, nx, nz, tr, cb), BF16),
            vmem((rank, cols), F32),
            vmem((rank, 2 * rank), F32),
            vmem((128, 256), F32),
            vmem((8, rank), F32),
            vmem((ny - 1, 8, rank), F32),
            sem((3, ny)),
            sem((3 + 2 * np,)), sem((3 + 2 * np,)),
            sem((1 + 2 * np, nx - 1)), sem((1 + 2 * np, nx - 1)),
            sem((9, ny - 1)), sem((9, ny - 1)),
            sem((2 + 2 * np, nz - 1)), sem((2 + 2 * np, nz - 1)),
            sem((2, nx * ny - 1)), sem((2, nx * ny - 1)),
        ],
        compiler_params=pltpu.CompilerParams(
            collective_id=0, has_side_effects=True, vmem_limit_bytes=VMEM_LIMIT),
        name="update",
    )(*(pltpu.with_memory_space_constraint(v, pltpu.MemorySpace.HBM) for v in args))


def factor8(cols):
    e = [[jnp.broadcast_to(cols[k][q:q + 1, :], (8, 128)) for k in range(q + 1)] for q in range(8)]
    low = [[None] * 8 for _ in range(8)]
    inv = [[None] * 8 for _ in range(8)]
    for p in range(8):
        inv[p][p] = lax.rsqrt(e[p][p])
        for q in range(p + 1, 8):
            low[q][p] = e[q][p] * inv[p][p]
        for q in range(p + 1, 8):
            for k in range(p + 1, q + 1):
                e[q][k] = e[q][k] - low[q][p] * low[k][p]
    for q in range(8):
        for k in range(q):
            acc = low[q][k] * inv[k][k]
            for m in range(k + 1, q):
                acc = acc + low[q][m] * inv[m][k]
            inv[q][k] = -acc * inv[q][q]
    return inv


def lanes(x, k):
    return jnp.broadcast_to(x[:, k:k + 1], (8, 128))


def rows8(x, k):
    return jnp.broadcast_to(x[k:k + 1, :], (8, 128))


def split3(x):
    high = x.astype(BF16).astype(F32)
    x = x - high
    mid = x.astype(BF16).astype(F32)
    return high, mid, x - mid


def rank8(a, v):
    ha, ma, la = split3(a)
    hv, mv, lv = split3(v)
    left = jnp.concatenate([ha, ma, la, ha, ma, ha], axis=0).astype(BF16)
    right_a = jnp.concatenate([ha, ha, ha, ma, ma, la], axis=0)
    right_v = jnp.concatenate([hv, hv, hv, mv, mv, lv], axis=0)
    return dot(left, jnp.concatenate([right_a, right_v], axis=1).astype(BF16), ((0,), (0,)))


def times_inverse(cols, inv):
    out = []
    for k in range(8):
        acc = cols[0] * inv[k][0]
        for j in range(1, k + 1):
            acc = acc + cols[j] * inv[k][j]
        out.append(acc)
    return out


def factor128(r, between):
    sub = lax.broadcasted_iota(jnp.int32, (8, 128), 0)
    a, v = r[0:8, 0:128], r[0:8, 128:256]
    cols = [lanes(a, k) for k in range(8)]
    last = None
    for s in range(16):
        if s in between:
            between[s][0](between[s][1])
        lo = 8 * s
        if s < 15:
            an, vn = r[lo + 8:lo + 16, 0:128], r[lo + 8:lo + 16, 128:256]
            if last is not None:
                low = times_inverse([lanes(an, lo - 8 + k) for k in range(8)], last[0])
                for k in range(8):
                    an = an - low[k] * rows8(last[1], k)
                    vn = vn - low[k] * rows8(last[2], k)
            below = [lanes(an, lo + k) for k in range(8)]
            ahead = [lanes(an, lo + 8 + k) for k in range(8)]
        inv = factor8(cols)
        new_a = new_v = None
        for k in range(8):
            m = jnp.where(sub == k, inv[k][k], 0.0)
            for q in range(k + 1, 8):
                m = jnp.where(sub == q, inv[q][k], m)
            ta, tv = m * rows8(a, k), m * rows8(v, k)
            new_a = ta if new_a is None else new_a + ta
            new_v = tv if new_v is None else new_v + tv
        r[lo:lo + 8, 128:256] = new_v
        if s < 15:
            low = times_inverse(below, inv)
            cols = []
            for k in range(8):
                an = an - low[k] * rows8(new_a, k)
                vn = vn - low[k] * rows8(new_v, k)
                acc = ahead[k]
                for j in range(8):
                    acc = acc - low[j] * rows8(low[j], k)
                cols.append(acc)
            a, v = an, vn
        last = inv, new_a, new_v
        if s < 13:
            r[lo + 24:128, :] = r[lo + 24:128, :] - rank8(new_a, new_v)[lo + 24:128, :]


def split(x):
    high = x.astype(BF16)
    return high, (x - high.astype(F32)).astype(BF16)


def outputs_kernel(orth, new_mom, nb_t, mom_hbm, basis_hbm, dir_hbm, basis_out, dir_out, sems):
    blocks, rows, wide = dir_out.shape
    factor = orth[...]
    copies = [pltpu.make_async_copy(new_mom, mom_hbm, sems.at[2, 0])]
    copies[0].start()
    for i in range(blocks):
        place = pl.ds(i * wide, wide)
        new_basis = nb_t[:, place]
        dir_out[i] = (math.sqrt(ROWS / RANK) * dot(factor, new_basis)).astype(BF16)
        basis_out[place, :] = new_basis.T
        for n, (src, dst) in enumerate((
            (dir_out.at[i], dir_hbm.at[:, place]),
            (basis_out.at[place, :], basis_hbm.at[place, :]),
        )):
            go = pltpu.make_async_copy(src, dst, sems.at[n, i])
            go.start()
            copies.append(go)
    for go in copies:
        go.wait()


def outputs_call(orth, new_mom, nb_t):
    rows, cols = new_mom.shape
    rank = orth.shape[1]
    wide = 256
    blocks = cols // wide
    space = pl.BlockSpec(memory_space=pltpu.VMEM)
    hbm = pl.BlockSpec(memory_space=pl.ANY)
    args = [pltpu.with_memory_space_constraint(v, pltpu.VMEM) for v in (orth, new_mom, nb_t)]
    return pl.pallas_call(
        outputs_kernel,
        out_shape=(
            jax.ShapeDtypeStruct((rows, cols), BF16),
            jax.ShapeDtypeStruct((cols, rank), BF16),
            jax.ShapeDtypeStruct((rows, cols), BF16),
        ),
        in_specs=[space] * 3,
        out_specs=(hbm,) * 3,
        scratch_shapes=[
            pltpu.VMEM((cols, rank), BF16),
            pltpu.VMEM((blocks, rows, wide), BF16),
            pltpu.SemaphoreType.DMA((3, blocks)),
        ],
        compiler_params=pltpu.CompilerParams(vmem_limit_bytes=VMEM_LIMIT),
        name="outputs",
    )(*args)


def per_device(momentum, gradient, old_basis):
    orth, new_momentum, basis_t = update_call(SHAPE, COLS, momentum, gradient, old_basis)
    return outputs_call(orth, new_momentum, basis_t)


def solution(mesh):
    in_specs = (P("zero", "tensor"), P("zero", "tensor"), P("tensor", None))
    out_specs = (P("zero", "tensor"), P("tensor", None), P("zero", "tensor"))
    return jax.shard_map(
        per_device, mesh=mesh, in_specs=in_specs, out_specs=out_specs, check_vma=False
    )
```
